128 devices in a mesh: blk: 16 (over y_hi, x, core), narrow: 8 (over z, y_lo).
Axes of the slice: x: 4, y: 4 (y_hi: 2, y_lo: 2; y = y_hi * 2 + y_lo), z: 4, core: 2. Of those that a mesh axis runs over, the one named last changes fastest.
Arguments:
- features: float32 [256, 131072], P('narrow', 'blk'), may hold values from -6 to 6
- degrees: int32 [131072], P('blk'), may hold values from 1 to 400
- tile_values: float32 [4096, 128, 128], P('blk'), may hold values from -24 to 24
- tile_list: int32 [16, 16, 3, 16], P('blk'), may hold values from 0 to 255, as said below
- tile_count: int32 [16, 16], P('blk'), may hold values from 0 to 16, as said below
- hub_local: int32 [16, 8], P('blk'), may hold values from 0 to 8191
- hub_weights: float32 [128, 131072], P(None, 'blk'), may hold values from -12 to 12
- weight: float32 [256, 256], replicated, may hold values from -0.375 to 0.375
- out_bias: float32 [256], replicated, may hold values from -3 to 3
Outputs:
- layer_out: float32 [256, 131072], P('narrow', 'blk')
The draws below stay inside these ranges and needn't reach their ends.
Inputs may be any that keep to these rules, and one draw needn't show every extreme that they name: `tile_list`: entries [:, :, 0, :] and [:, :, 1, :] lie below 64; for each target device the entries [d, :, 2, :] are the numbers 0 to 255, each once. `tile_count`: every target device has at least one source device with exactly 16 live slots.
All inputs are finite; a program needn't handle non-finite values.
Results may differ from the reference program's by a relative error of at most 0.0003.
Values sent between devices are 32-bit elements; how exact they have to be, the bound alone decides.
A program may use at most 128 MiB of HBM per device.

```python
import jax
import jax.numpy as jnp
from jax import lax

H = 256
TILE = 128
RB = 64
SLOTS = 16
HUB_DEV = 8
NODE_DEV = 8192
NODES = 131072
TV = 256
HUBS = 128
N_BLK = 16


def draw_permuted(key_one):
    return jax.random.permutation(key_one, N_BLK * SLOTS)


def draw_tile_list(key, part):
    key = jax.random.fold_in(key, 11)
    key_rows, key_cols, key_perm = jax.random.split(key, 3)
    row_draw = jax.random.randint(key_rows, (N_BLK, N_BLK, SLOTS), 0, RB)
    col_draw = jax.random.randint(key_cols, (N_BLK, N_BLK, SLOTS), 0, RB)
    sub_keys = jax.random.split(key_perm, N_BLK)
    perm_draw = jax.vmap(draw_permuted)(sub_keys).reshape(N_BLK, N_BLK, SLOTS).astype(jnp.int32)
    return jnp.stack([row_draw.astype(jnp.int32), col_draw.astype(jnp.int32), perm_draw], axis=2).astype(jnp.int32)


def draw_tile_count(key, part):
    key = jax.random.fold_in(key, 23)
    key_count, key_full = jax.random.split(key)
    count_draw = jax.random.randint(key_count, (N_BLK, N_BLK), 0, SLOTS + 1)
    full_owner = jax.random.randint(key_full, (N_BLK,), 0, N_BLK)
    is_full = jnp.arange(N_BLK, dtype=jnp.int32)[None, :] == full_owner[:, None]
    return jnp.where(is_full, SLOTS, count_draw).astype(jnp.int32)


def touch_ends(array, rng, low, high):
    extent = array.shape
    place = [jax.random.randint(jax.random.fold_in(rng, axis), (), 0, extent[axis]) for axis in range(len(extent))]
    array = array.at[tuple(place)].set(low)
    longest = extent.index(max(extent))
    place[longest] = (place[longest] + 1) % extent[longest]
    return array.at[tuple(place)].set(high)


def level_of(key, dims, pieces, smallest, high):
    factor_of = 1.0
    for axis_at, shards_of in pieces:
        draws = jax.random.uniform(jax.random.fold_in(jax.random.fold_in(key, 6), axis_at), (shards_of,), jnp.float32, smallest / len(pieces), high / len(pieces))
        factor_of = factor_of * jnp.repeat(jnp.exp(draws), dims[axis_at] // shards_of).reshape((-1,) + (1,) * (len(dims) - 1 - axis_at))
    return factor_of


def centred(rng, dims, deviation, bound, shards=(), kind=jnp.bfloat16):
    array = deviation * jax.random.normal(rng, dims, jnp.float32)
    if shards:
        array = array * level_of(rng, dims, shards, -0.22, 0.18)
    return jnp.clip(array, -bound, bound).astype(kind)


def setup_inputs(seed: int = 0) -> dict:
    seeds = jax.random.split(jax.random.key(seed), 10)
    return {
        "features": centred(seeds[0], (H, NODES), 1.0, 6.0, ((0, 8), (1, 16)), jnp.float32),
        "degrees": touch_ends(jax.random.randint(seeds[1], (NODES,), 1, 401), jax.random.fold_in(seeds[1], 1), 1, 400).astype(jnp.int32),
        "tile_values": centred(seeds[2], (TV * N_BLK, TILE, TILE), 4.0, 24.0, ((0, 16),), jnp.float32),
        "tile_list": draw_tile_list(jax.random.fold_in(seeds[9], 71), 0),
        "tile_count": draw_tile_count(jax.random.fold_in(seeds[9], 71), 0),
        "hub_local": touch_ends(jax.random.randint(seeds[5], (N_BLK, HUB_DEV), 0, NODE_DEV), jax.random.fold_in(seeds[5], 1), 0, NODE_DEV - 1).astype(jnp.int32),
        "hub_weights": centred(seeds[6], (HUBS, NODES), 2.0, 12.0, ((1, 16),), jnp.float32),
        "weight": centred(seeds[7], (H, H), H ** -0.5, 0.375, (), jnp.float32),
        "out_bias": centred(seeds[8], (H,), 0.5, 3.0, (), jnp.float32),
    }


def reference(features, degrees, tile_values, tile_list, tile_count, hub_local, hub_weights, weight, out_bias):
    inv_root = lax.rsqrt(degrees.astype(jnp.float32))
    scaled = features * inv_root[None, :]
    x_blocks = scaled.reshape(H, N_BLK * RB, TILE)
    by_device = tile_values.reshape(N_BLK, SLOTS * N_BLK, TILE, TILE)
    owners = jnp.arange(N_BLK, dtype=jnp.int32)
    slot_pos = jnp.arange(SLOTS, dtype=jnp.int32)
    block_ids = jnp.arange(RB, dtype=jnp.int32)

    def one_device(device):
        tile_lists = tile_list[device]
        slot_counts = tile_count[device]
        row_ids = tile_lists[:, 0, :].reshape(-1)
        col_ids = (tile_lists[:, 1, :] + owners[:, None] * RB).reshape(-1).astype(jnp.int32)
        tile_ids = tile_lists[:, 2, :].reshape(-1)
        is_live = (slot_pos[None, :] < slot_counts[:, None]).reshape(-1)
        src_blocks = jnp.take(x_blocks, col_ids, axis=1)
        picked = jnp.take(by_device[device], tile_ids, axis=0)
        products = jnp.einsum('csj,sij->sci', src_blocks, picked, precision=lax.Precision.HIGHEST)
        chooser = ((row_ids[:, None] == block_ids[None, :]) & is_live[:, None]).astype(jnp.float32)
        return jnp.einsum('sci,sr->cri', products, chooser, precision=lax.Precision.HIGHEST)
    per_device = lax.map(one_device, owners)
    tile_sum = jnp.transpose(per_device, (1, 0, 2, 3)).reshape(H, N_BLK * RB * TILE)
    hub_ids = (hub_local + owners[:, None] * (RB * TILE)).reshape(-1).astype(jnp.int32)
    hub_sum = jnp.dot(jnp.take(scaled, hub_ids, axis=1), hub_weights, precision=lax.Precision.HIGHEST)
    aggregated = inv_root[None, :] * (tile_sum + hub_sum + scaled)
    return jax.nn.relu(jnp.dot(weight.T, aggregated, precision=lax.Precision.HIGHEST) + out_bias[:, None])
```

```python
import functools

import jax
import jax.numpy as jnp
from jax import lax
from jax.experimental import pallas as pl
from jax.experimental.pallas import tpu as pltpu
from jax.sharding import PartitionSpec as P

TILE = 128
SLOTS = 16
F = 4
BLOCKS = 64
TV = 256
GROUP = 8
MESH = pl.DeviceIdType.MESH
ROW = ((1, 0), (3, 0), (1, 1), (3, 1), (2, 0), (2, 1), (0, 1))
NARROW = ((1, 0), (3, 0), (0, 1), (2, 0), (1, 1), (3, 1), (2, 1))


def split(x):
    hi = x.astype(jnp.bfloat16)
    lo = (x - hi.astype(jnp.float32)).astype(jnp.bfloat16)
    return hi, lo


def nt_dot(a, b):
    return lax.dot_general(a, b, (((1,), (1,)), ((), ())), preferred_element_type=jnp.float32)


def nn_dot(a, b):
    return jnp.dot(a, b, preferred_element_type=jnp.float32)


def exchange_kernel(
    feat, deg, weight, cols, hubs,
    recv, y_out, hub_out,
    xt, ysend, ya, yb, yc, yd, pa, pb, pc, pd, own_b, par_b, lists_v, lists_s, hub_v,
    s1, r1, s2, r2, sy, ry, sl, rl, sh, rh, so, sp, rr, loc,
):
    y4, yp = (ya, yb, yc, yd), (pa, pb, pc, pd)
    blk = lax.axis_index("blk")
    nar = lax.axis_index("narrow")
    yh, x, core = blk // 8, (blk // 2) % 4, blk % 2
    z, yl = nar // 2, nar % 2
    partner = (1 - yh) * 8 + x * 2 + core

    def row_peer(step, other):
        return yh * 8 + lax.rem(x + step, 4) * 2 + lax.rem(core + other, 2)

    def narrow_peer(step, other):
        return lax.rem(z + step, 4) * 2 + lax.rem(yl + other, 2)

    bar = pltpu.get_barrier_semaphore()
    for j in range(1, 16):
        pl.semaphore_signal(bar, inc=1, device_id=(lax.rem(blk + j, 16), nar), device_id_type=MESH)
    for step, other in NARROW:
        pl.semaphore_signal(
            bar, inc=1, device_id=(blk, narrow_peer(step, other)), device_id_type=MESH
        )
    pl.semaphore_wait(bar, 22)

    def send1(n, to):
        return pltpu.make_async_remote_copy(
            src_ref=feat.at[:, pl.ds(pl.multiple_of(to * 1024, 1024), 1024)],
            dst_ref=xt.at[pl.ds(pl.multiple_of(n * 32, 32), 32), :],
            send_sem=s1.at[to], recv_sem=r1.at[n],
            device_id=(blk, to), device_id_type=MESH,
        )

    for step, other in NARROW:
        send1(nar, narrow_peer(step, other)).start()
    own1 = pltpu.make_async_copy(
        feat.at[:, pl.ds(pl.multiple_of(nar * 1024, 1024), 1024)],
        xt.at[pl.ds(pl.multiple_of(nar * 32, 32), 32), :], loc.at[0],
    )
    own1.start()

    def send_list(step, other):
        slot = step * 2 + other
        return pltpu.make_async_remote_copy(
            src_ref=cols, dst_ref=lists_v.at[slot], send_sem=sl.at[slot], recv_sem=rl.at[slot],
            device_id=(row_peer(4 - step, other), nar), device_id_type=MESH,
        )

    for step, other in ROW:
        send_list(step, other).start()
    lists_v[0] = cols[...]
    for step, other in ROW:
        send_list(step, other).wait()
    to_smem = pltpu.make_async_copy(lists_v, lists_s, loc.at[1])
    to_smem.start()

    wh, wl = split(weight[...].T)
    inv = lax.rsqrt(deg[pl.ds(pl.multiple_of(nar * 8, 8), 8), :].astype(jnp.float32))
    to_smem.wait()
    own1.wait()
    for step, other in NARROW:
        send1(narrow_peer(step, other), narrow_peer(step, other)).wait_recv()

    for b in range(8):
        xh, xl = split(xt[:, b * TILE : (b + 1) * TILE])
        y = nn_dot(wh, xh) + nn_dot(wl, xh) + nn_dot(wh, xl)
        y = y * inv[b : b + 1, :]
        for n in range(8):
            for f in range(F):
                row = n * 32 + f * 8
                ysend[f, n, b] = y[row : row + 8, :]

    def send2(f, n, to):
        return pltpu.make_async_remote_copy(
            src_ref=ysend.at[f, to],
            dst_ref=y4[f].at[pl.ds(pl.multiple_of(n * 8, 8), 8)],
            send_sem=s2.at[f, to], recv_sem=r2.at[f, n],
            device_id=(blk, to), device_id_type=MESH,
        )

    def own2(f):
        return pltpu.make_async_copy(
            ysend.at[f, nar], y4[f].at[pl.ds(pl.multiple_of(nar * 8, 8), 8)], loc.at[2 + f]
        )

    for f in range(F):
        for step, other in NARROW:
            send2(f, nar, narrow_peer(step, other)).start()
        own2(f).start()

    def send_y(f):
        return pltpu.make_async_remote_copy(
            src_ref=y4[f], dst_ref=yp[f], send_sem=sy.at[f], recv_sem=ry.at[f],
            device_id=(partner, nar), device_id_type=MESH,
        )

    def send_blocks(buf, sem, f, source, step, other):
        slot = step * 2 + other
        return pltpu.make_async_remote_copy(
            src_ref=buf.at[f, slot], dst_ref=recv.at[f, source],
            send_sem=sem.at[f, slot], recv_sem=rr.at[f, source],
            device_id=(row_peer(step, other), nar), device_id_type=MESH,
        )

    def keep_blocks(buf, f, source, sem):
        return pltpu.make_async_copy(buf.at[f, 0], recv.at[f, source], sem)

    def pack(src, buf, f, source, slot):
        for k in range(SLOTS):
            c = lists_s[slot, source // 8, lax.rem(source, 8) * SLOTS + k]
            buf[f, slot, k] = src[f][c]

    for f in range(F):
        own2(f).wait()
        for step, other in NARROW:
            n = narrow_peer(step, other)
            send2(f, n, n).wait_recv()
        send_y(f).start()
        for step, other in ROW:
            pack(y4, own_b, f, blk, step * 2 + other)
            send_blocks(own_b, so, f, blk, step, other).start()
        pack(y4, own_b, f, blk, 0)
        keep_blocks(own_b, f, blk, loc.at[6 + f]).start()

    lane = lax.broadcasted_iota(jnp.int32, (8, TILE), 1)
    hub = jnp.zeros((8, TILE), jnp.float32)
    for h in range(8):
        node = hubs[h]
        here = lane == lax.rem(node, TILE)
        for f in range(F):
            column = jnp.sum(jnp.where(here, y4[f][node // TILE], 0.0), axis=1, keepdims=True)
            hub = jnp.where(lane == f * 8 + h, column, hub)
    hub_v[...] = hub

    def send_hub(source, to):
        return pltpu.make_async_remote_copy(
            src_ref=hub_v, dst_ref=hub_out.at[source], send_sem=sh.at[to], recv_sem=rh.at[source],
            device_id=(to, nar), device_id_type=MESH,
        )

    for j in range(1, 16):
        send_hub(blk, lax.rem(blk + j, 16)).start()
    keep_hub = pltpu.make_async_copy(hub_v, hub_out.at[blk], loc.at[14])
    keep_hub.start()
    keep_y = [pltpu.make_async_copy(y4[f], y_out.at[f], loc.at[15 + f]) for f in range(F)]
    for f in range(F):
        keep_y[f].start()

    for f in range(F):
        send_y(f).wait_recv()
        for step, other in ROW:
            pack(yp, par_b, f, partner, step * 2 + other)
            send_blocks(par_b, sp, f, partner, step, other).start()
        pack(yp, par_b, f, partner, 0)
        keep_blocks(par_b, f, partner, loc.at[10 + f]).start()

    for f in range(F):
        for step, other in ROW:
            peer = row_peer(step, other)
            send_blocks(own_b, so, f, peer, step, other).wait()
            other_row = lax.rem(peer + 8, 16)
            send_blocks(par_b, sp, f, other_row, step, other).wait()
        keep_blocks(own_b, f, blk, loc.at[6 + f]).wait()
        keep_blocks(par_b, f, partner, loc.at[10 + f]).wait()
        send_y(f).wait_send()
        for step, other in NARROW:
            n = narrow_peer(step, other)
            send2(f, n, n).wait_send()
    for step, other in NARROW:
        n = narrow_peer(step, other)
        send1(n, n).wait_send()
    for j in range(1, 16):
        peer = lax.rem(blk + j, 16)
        send_hub(peer, peer).wait()
    keep_hub.wait()
    for f in range(F):
        keep_y[f].wait()


def exchange(feat, deg, weight, cols, hubs):
    f32 = jnp.float32
    dma = pltpu.SemaphoreType.DMA
    vmem = pl.BlockSpec(memory_space=pltpu.VMEM)
    smem = pl.BlockSpec(memory_space=pltpu.SMEM)
    hbm = pl.BlockSpec(memory_space=pl.ANY)
    return pl.pallas_call(
        exchange_kernel,
        out_shape=(
            jax.ShapeDtypeStruct((F, 16, SLOTS, 8, TILE), f32),
            jax.ShapeDtypeStruct((F, BLOCKS, 8, TILE), f32),
            jax.ShapeDtypeStruct((16, 8, TILE), f32),
        ),
        in_specs=[hbm, vmem, vmem, vmem, smem],
        out_specs=(hbm, hbm, hbm),
        scratch_shapes=[
            pltpu.VMEM((256, 1024), f32),
            pltpu.VMEM((F, 8, 8, 8, TILE), f32),
            *[pltpu.VMEM((BLOCKS, 8, TILE), f32)] * 8,
            pltpu.VMEM((F, 8, SLOTS, 8, TILE), f32),
            pltpu.VMEM((F, 8, SLOTS, 8, TILE), f32),
            pltpu.VMEM((8, 8, TILE), jnp.int32),
            pltpu.SMEM((8, 8, TILE), jnp.int32),
            pltpu.VMEM((8, TILE), f32),
            dma((8,)), dma((8,)),
            dma((F, 8)), dma((F, 8)),
            dma((F,)), dma((F,)),
            dma((8,)), dma((8,)),
            dma((16,)), dma((16,)),
            dma((F, 8)), dma((F, 8)), dma((F, 16)),
            dma((20,)),
        ],
        compiler_params=pltpu.CompilerParams(
            collective_id=0, has_side_effects=True, vmem_limit_bytes=32 * 2**20
        ),
    )(feat, deg, weight, cols, hubs)


def tile_kernel(
    recv, y4, hub_in, deg, bias, hub_w, lists, counts, tiles,
    out,
    acc, tbuf, hw_buf, src_s, row_s, buf_s, sem, hw_sem,
):
    fetch_hw = pltpu.make_async_copy(hub_w, hw_buf, hw_sem)
    fetch_hw.start()

    def fetch(t, pos):
        return pltpu.make_async_copy(tiles.at[t], tbuf.at[pos], sem.at[pos])

    def source(o, pos):
        def slot(k, pos):
            src_s[pos] = o * SLOTS + k
            row_s[pos] = lists[o * 3, k]
            buf_s[pos] = pos
            fetch(lists[o * 3 + 2, k], pos).start()
            return pos + 1

        return lax.fori_loop(0, counts[0, o], slot, pos)

    live = lax.fori_loop(0, 16, source, jnp.int32(0))
    for j in range(GROUP):
        src_s[live + j] = 0
        row_s[live + j] = BLOCKS
        buf_s[live + j] = 0

    lane = lax.broadcasted_iota(jnp.int32, (8, TILE), 1)
    hub = []
    for f in range(F):
        total = jnp.zeros((8, TILE), jnp.float32)
        for o in range(16):
            moved = pltpu.roll(hub_in[o], (o * 8 - f * 8) % TILE, 1)
            total = jnp.where(lane // 8 == o, moved, total)
        hub.append(total)
    gh, gl = split(jnp.concatenate(hub, axis=0))
    g2 = jnp.concatenate([gh, gl], axis=0)
    fetch_hw.wait()

    def base(i, carry):
        hh, hl = split(hw_buf[:, pl.ds(pl.multiple_of(i * 512, 512), 512)])
        p = nn_dot(g2, hh)
        p = p[:32] + p[32:] + nn_dot(gh, hl)
        for b in range(4):
            for f in range(F):
                acc[i * 4 + b, f] = (
                    p[f * 8 : f * 8 + 8, b * TILE : (b + 1) * TILE] + y4[f, i * 4 + b]
                )
        return carry

    lax.fori_loop(0, 16, base, 0)

    def group(g, carry):
        first = g * GROUP
        for j in range(GROUP):
            @pl.when(first + j < live)
            def _():
                fetch(0, first + j).wait()

        products = []
        for j in range(GROUP):
            s = src_s[first + j]
            xs = jnp.concatenate([recv[f, s] for f in range(F)], axis=0)
            xh, xl = split(xs)
            th, tl = split(tbuf[buf_s[first + j]])
            p = nt_dot(jnp.concatenate([xh, xl], axis=0), th)
            products.append(p[:32] + p[32:] + nt_dot(xh, tl))
        for j in range(GROUP):
            r = row_s[first + j]
            for f in range(F):
                acc[r, f] += products[j][f * 8 : f * 8 + 8, :]
        return carry

    lax.fori_loop(0, (live + GROUP - 1) // GROUP, group, 0)

    def finish(i, carry):
        inv = lax.rsqrt(deg[pl.ds(pl.multiple_of(i * 8, 8), 8), :].astype(jnp.float32))
        for b in range(8):
            for f in range(F):
                value = acc[i * 8 + b, f] * inv[b : b + 1, :] + bias[f * 8 : f * 8 + 8, :]
                out[f * 8 : f * 8 + 8, pl.ds(pl.multiple_of((i * 8 + b) * TILE, TILE), TILE)] = (
                    jnp.maximum(value, 0.0)
                )
        return carry

    lax.fori_loop(0, 8, finish, 0)


def tile_sums(recv, y4, hub_in, deg, bias, hub_w, lists, counts, tiles):
    f32 = jnp.float32
    vmem = pl.BlockSpec(memory_space=pltpu.VMEM)
    smem = pl.BlockSpec(memory_space=pltpu.SMEM)
    hbm = pl.BlockSpec(memory_space=pl.ANY)
    return pl.pallas_call(
        tile_kernel,
        out_shape=jax.ShapeDtypeStruct((32, BLOCKS * TILE), f32),
        in_specs=[vmem, vmem, vmem, vmem, vmem, hbm, smem, smem, hbm],
        out_specs=vmem,
        scratch_shapes=[
            pltpu.VMEM((BLOCKS + 1, F, 8, TILE), f32),
            pltpu.VMEM((TV, TILE, TILE), f32),
            pltpu.VMEM((128, BLOCKS * TILE), f32),
            pltpu.SMEM((TV + GROUP,), jnp.int32),
            pltpu.SMEM((TV + GROUP,), jnp.int32),
            pltpu.SMEM((TV + GROUP,), jnp.int32),
            pltpu.SemaphoreType.DMA((TV,)),
            pltpu.SemaphoreType.DMA,
        ],
        compiler_params=pltpu.CompilerParams(vmem_limit_bytes=48 * 2**20),
    )(recv, y4, hub_in, deg, bias, hub_w, lists, counts, tiles)


def body(
    features, degrees, tile_values, tile_list, tile_count, hub_local, hub_weights, weight, out_bias
):
    deg = degrees.reshape(BLOCKS, TILE)
    cols = jnp.pad(tile_list[0, :, 1, :].reshape(2, TILE), ((0, 6), (0, 0)))
    recv, y4, hub = exchange(features, deg, weight, cols, hub_local.reshape(8))
    mine = lax.dynamic_slice_in_dim(out_bias, lax.axis_index("narrow") * 32, 32)
    bias = jnp.broadcast_to(mine[:, None], (32, TILE))
    return tile_sums(
        recv.reshape(F, 16 * SLOTS, 8, TILE), y4, hub, deg, bias, hub_weights,
        tile_list.reshape(48, SLOTS), tile_count, tile_values,
    )


def solution(mesh):
    return jax.shard_map(
        body,
        mesh=mesh,
        in_specs=(
            P("narrow", "blk"),
            P("blk"),
            P("blk", None, None),
            P("blk", None, None, None),
            P("blk", None),
            P("blk", None),
            P(None, "blk"),
            P(),
            P(),
        ),
        out_specs=P("narrow", "blk"),
        check_vma=False,
    )
```

```python
import functools

import jax
import jax.numpy as jnp
from jax import lax
from jax.experimental import pallas as pl
from jax.experimental.pallas import tpu as pltpu
from jax.sharding import PartitionSpec as P

TILE = 128
SLOTS = 16
F = 4
BLOCKS = 64
TV = 256
MESH = pl.DeviceIdType.MESH
ROW = ((1, 0), (3, 0), (1, 1), (3, 1), (2, 0), (2, 1), (0, 1))
NARROW = ((1, 0), (3, 0), (0, 1), (2, 0), (1, 1), (3, 1), (2, 1))


def split(x):
    hi = x.astype(jnp.bfloat16)
    lo = (x - hi.astype(jnp.float32)).astype(jnp.bfloat16)
    return hi, lo


def nt_dot(a, b):
    return lax.dot_general(a, b, (((1,), (1,)), ((), ())), preferred_element_type=jnp.float32)


def nn_dot(a, b):
    return jnp.dot(a, b, preferred_element_type=jnp.float32)


def exchange_kernel(
    feat, deg, weight, lists, my_list, hubs, tiles, hub_w,
    prod_own, prod_par, base_out,
    xt, ysend, ya, yb, yc, yd, pa, pb, pc, pd, own_b, early_b, late_b,
    got_own, got_early, got_late, lists_v, lists_s, hub_v, hub_in, deg_v, w_v, t_v, hw_v,
    p_own, p_par, base,
    s1, r1, s2, r2, sy, ry, sl, rl, sh, rh, so, ro, se, re, sq, rq, loc,
):
    y4, yp = (ya, yb, yc, yd), (pa, pb, pc, pd)
    blk = lax.axis_index("blk")
    nar = lax.axis_index("narrow")
    yh, x, core = blk // 8, (blk // 2) % 4, blk % 2
    z, yl = nar // 2, nar % 2
    me = x * 2 + core
    partner = (1 - yh) * 8 + me

    def row_peer(step, other):
        return lax.rem(x + step, 4) * 2 + lax.rem(core + other, 2)

    def narrow_peer(step, other):
        return lax.rem(z + step, 4) * 2 + lax.rem(yl + other, 2)

    bar = pltpu.get_barrier_semaphore()
    for step, other in NARROW:
        pl.semaphore_signal(
            bar, inc=1, device_id=(blk, narrow_peer(step, other)), device_id_type=MESH
        )
    for step, other in ROW:
        pl.semaphore_signal(
            bar, inc=1, device_id=(yh * 8 + row_peer(step, other), nar), device_id_type=MESH
        )
    pl.semaphore_signal(bar, inc=1, device_id=(partner, nar), device_id_type=MESH)

    get_deg = pltpu.make_async_copy(deg, deg_v, loc.at[0])
    get_w = pltpu.make_async_copy(weight, w_v, loc.at[1])
    get_own = pltpu.make_async_copy(
        feat.at[:, pl.ds(pl.multiple_of(nar * 1024, 1024), 1024)],
        xt.at[pl.ds(pl.multiple_of(nar * 32, 32), 32), :], loc.at[2],
    )
    get_list = pltpu.make_async_copy(lists.at[0], lists_v.at[0], loc.at[3])
    get_t = pltpu.make_async_copy(tiles, t_v, loc.at[4])
    get_hw = pltpu.make_async_copy(hub_w, hw_v, loc.at[5])
    for copy in (get_w, get_deg, get_own, get_list):
        copy.start()
    pl.semaphore_wait(bar, 15)

    def send1(n, to):
        return pltpu.make_async_remote_copy(
            src_ref=feat.at[:, pl.ds(pl.multiple_of(to * 1024, 1024), 1024)],
            dst_ref=xt.at[pl.ds(pl.multiple_of(n * 32, 32), 32), :],
            send_sem=s1.at[to], recv_sem=r1.at[n],
            device_id=(blk, to), device_id_type=MESH,
        )

    for step, other in NARROW:
        send1(nar, narrow_peer(step, other)).start()

    def send_list(step, other):
        slot = step * 2 + other
        return pltpu.make_async_remote_copy(
            src_ref=lists.at[0], dst_ref=lists_v.at[slot],
            send_sem=sl.at[slot], recv_sem=rl.at[slot],
            device_id=(yh * 8 + row_peer(4 - step, other), nar), device_id_type=MESH,
        )

    for step, other in ROW:
        send_list(step, other).start()
    get_t.start()
    get_hw.start()

    get_w.wait()
    get_deg.wait()
    wh, wl = split(w_v[...].T)
    inv = lax.rsqrt(deg_v[pl.ds(pl.multiple_of(nar * 8, 8), 8), :].astype(jnp.float32))
    get_own.wait()
    for step, other in NARROW:
        n = narrow_peer(step, other)
        send1(n, n).wait_recv()

    for b in range(8):
        xh, xl = split(xt[:, b * TILE : (b + 1) * TILE])
        y = nn_dot(wh, xh) + nn_dot(wl, xh) + nn_dot(wh, xl)
        y = y * inv[b : b + 1, :]
        for n in range(8):
            for f in range(F):
                row = n * 32 + f * 8
                ysend[f, n, b] = y[row : row + 8, :]

    def send2(f, n, to):
        return pltpu.make_async_remote_copy(
            src_ref=ysend.at[f, to],
            dst_ref=y4[f].at[pl.ds(pl.multiple_of(n * 8, 8), 8)],
            send_sem=s2.at[f, to], recv_sem=r2.at[f, n],
            device_id=(blk, to), device_id_type=MESH,
        )

    def own2(f):
        return pltpu.make_async_copy(
            ysend.at[f, nar], y4[f].at[pl.ds(pl.multiple_of(nar * 8, 8), 8)], loc.at[6 + f]
        )

    for f in range(F):
        for step, other in NARROW:
            send2(f, nar, narrow_peer(step, other)).start()
        own2(f).start()

    get_list.wait()
    for step, other in ROW:
        send_list(step, other).wait_recv()
    to_smem = pltpu.make_async_copy(lists_v, lists_s, loc.at[10])
    to_smem.start()
    to_smem.wait()

    def send_y(f):
        return pltpu.make_async_remote_copy(
            src_ref=y4[f], dst_ref=yp[f], send_sem=sy.at[f], recv_sem=ry.at[f],
            device_id=(partner, nar), device_id_type=MESH,
        )

    def send_blocks(buf, got, ssem, rsem, part, source, step, other):
        slot = step * 2 + other
        return pltpu.make_async_remote_copy(
            src_ref=buf.at[part, slot], dst_ref=got.at[part, source],
            send_sem=ssem.at[part, slot], recv_sem=rsem.at[part, source],
            device_id=(yh * 8 + row_peer(step, other), nar), device_id_type=MESH,
        )

    def column(slot, source, k):
        return lists_s[slot, source, 1, k]

    def send_own(f, source, step, other):
        return send_blocks(own_b, got_own, so, ro, f, source, step, other)

    def send_early(f, source, step, other):
        return send_blocks(early_b, got_early, se, re, f, source, step, other)

    def send_late(q, source, step, other):
        return send_blocks(late_b, got_late, sq, rq, q, source, step, other)

    for f in range(F):
        own2(f).wait()
        for step, other in NARROW:
            n = narrow_peer(step, other)
            send2(f, n, n).wait_recv()
        send_y(f).start()
        for step, other in ROW:
            slot = step * 2 + other
            for k in range(SLOTS):
                own_b[f, slot, k] = y4[f][column(slot, blk, k)]
            send_own(f, me, step, other).start()
        for k in range(SLOTS):
            got_own[f, me, k] = y4[f][column(0, blk, k)]

    lane = lax.broadcasted_iota(jnp.int32, (8, TILE), 1)
    hub = jnp.zeros((8, TILE), jnp.float32)
    for h in range(8):
        node = hubs[0, h]
        here = lane == lax.rem(node, TILE)
        for f in range(F):
            col = jnp.sum(jnp.where(here, y4[f][node // TILE], 0.0), axis=1, keepdims=True)
            hub = jnp.where(lane == f * 8 + h, col, hub)
    hub_v[...] = hub
    hub_in[blk] = hub

    def swap_hub(source):
        return pltpu.make_async_remote_copy(
            src_ref=hub_v, dst_ref=hub_in.at[source], send_sem=sh.at[16], recv_sem=rh.at[source],
            device_id=(partner, nar), device_id_type=MESH,
        )

    def send_hub(src, source, sem, step, other):
        return pltpu.make_async_remote_copy(
            src_ref=src, dst_ref=hub_in.at[source], send_sem=sh.at[sem],
            recv_sem=rh.at[source],
            device_id=(yh * 8 + row_peer(step, other), nar), device_id_type=MESH,
        )

    swap_hub(blk).start()
    for step, other in ROW:
        send_hub(hub_v, blk, step * 2 + other, step, other).start()

    for f in range(2):
        send_y(f).wait_recv()
        for step, other in ROW:
            slot = step * 2 + other
            for k in range(SLOTS):
                early_b[f, slot, k] = yp[f][column(slot, partner, k)]
            send_early(f, me, step, other).start()
        for k in range(SLOTS):
            got_early[f, me, k] = yp[f][column(0, partner, k)]

    swap_hub(partner).wait_recv()
    for step, other in ROW:
        send_hub(hub_in.at[partner], partner, 8 + step * 2 + other, step, other).start()

    for f in range(2, F):
        send_y(f).wait_recv()
    for q in range(4):
        for step, other in ROW:
            slot = step * 2 + other
            for k in range(4):
                c = column(slot, partner, q * 4 + k)
                for f in range(2):
                    late_b[q, slot, f, k] = yp[2 + f][c]
            send_late(q, me, step, other).start()
        for k in range(4):
            c = column(0, partner, q * 4 + k)
            for f in range(2):
                got_late[q, me, f, k] = yp[2 + f][c]

    for step, other in ROW:
        peer = row_peer(step, other)
        for o in (yh * 8 + peer, (1 - yh) * 8 + peer):
            send_hub(hub_v, o, 0, step, other).wait_recv()
    parts = []
    for f in range(F):
        total = jnp.zeros((8, TILE), jnp.float32)
        for o in range(16):
            moved = pltpu.roll(hub_in[o], (o * 8 - f * 8) % TILE, 1)
            total = jnp.where(lane // 8 == o, moved, total)
        parts.append(total)
    gh, gl = split(jnp.concatenate(parts, axis=0))
    g2 = jnp.concatenate([gh, gl], axis=0)
    get_hw.wait()

    def hub_sum(i, carry):
        hh, hl = split(hw_v[:, pl.ds(pl.multiple_of(i * 512, 512), 512)])
        p = nn_dot(g2, hh)
        p = p[:32] + p[32:] + nn_dot(gh, hl)
        for b in range(4):
            for f in range(F):
                base[i * 4 + b, f] = (
                    p[f * 8 : f * 8 + 8, b * TILE : (b + 1) * TILE] + y4[f][i * 4 + b]
                )
        return carry

    lax.fori_loop(0, 16, hub_sum, 0)
    put_base = pltpu.make_async_copy(base, base_out, loc.at[16])
    put_base.start()

    get_t.wait()

    def product(xs, t):
        xh, xl = split(xs)
        th, tl = split(t_v[t])
        p = nt_dot(jnp.concatenate([xh, xl], axis=0), th)
        return p[:32] + p[32:] + nt_dot(xh, tl)

    for f in range(F):
        for step, other in ROW:
            send_own(f, row_peer(step, other), step, other).wait()

    def own_products(i, carry):
        for k in range(SLOTS):
            xs = jnp.concatenate([got_own[f, i, k] for f in range(F)], axis=0)
            p = product(xs, my_list[0, yh * 8 + i, 2, k])
            for f in range(F):
                p_own[i, k, f] = p[f * 8 : f * 8 + 8, :]
        return carry

    lax.fori_loop(0, 8, own_products, 0)
    put_own = pltpu.make_async_copy(p_own, prod_own, loc.at[11])
    put_own.start()

    for f in range(F):
        send_y(f).wait_send()
        for step, other in NARROW:
            n = narrow_peer(step, other)
            send2(f, n, n).wait_send()
    for step, other in NARROW:
        n = narrow_peer(step, other)
        send1(n, n).wait_send()
    for step, other in ROW:
        send_list(step, other).wait_send()
    swap_hub(partner).wait_send()
    for step, other in ROW:
        send_hub(hub_v, blk, step * 2 + other, step, other).wait_send()
        send_hub(hub_v, blk, 8 + step * 2 + other, step, other).wait_send()
    for f in range(2):
        for step, other in ROW:
            send_early(f, row_peer(step, other), step, other).wait()

    def put_par(q):
        return pltpu.make_async_copy(p_par.at[q], prod_par.at[q], loc.at[12 + q])

    for q in range(4):
        for step, other in ROW:
            send_late(q, row_peer(step, other), step, other).wait()

        def par_products(i, carry):
            for j in range(2):
                for k in range(4):
                    xs = jnp.concatenate(
                        [got_early[f, i * 2 + j, q * 4 + k] for f in range(2)]
                        + [got_late[q, i * 2 + j, f, k] for f in range(2)],
                        axis=0,
                    )
                    t = my_list[0, (1 - yh) * 8 + i * 2 + j, 2, q * 4 + k]
                    p = product(xs, t)
                    for f in range(F):
                        p_par[q, i * 2 + j, k, f] = p[f * 8 : f * 8 + 8, :]
            return carry

        lax.fori_loop(0, 4, par_products, 0)
        put_par(q).start()

    put_own.wait()
    put_base.wait()
    for q in range(4):
        put_par(q).wait()


def exchange(feat, deg, weight, lists, hubs, tiles, hub_w):
    f32 = jnp.float32
    dma = pltpu.SemaphoreType.DMA
    vmem = pltpu.VMEM
    smem = pl.BlockSpec(memory_space=pltpu.SMEM)
    hbm = pl.BlockSpec(memory_space=pl.ANY)
    tile = (8, TILE)
    return pl.pallas_call(
        exchange_kernel,
        out_shape=(
            jax.ShapeDtypeStruct((8, SLOTS, F, *tile), f32),
            jax.ShapeDtypeStruct((4, 8, 4, F, *tile), f32),
            jax.ShapeDtypeStruct((BLOCKS, F, *tile), f32),
        ),
        in_specs=[hbm, hbm, hbm, hbm, smem, smem, hbm, hbm],
        out_specs=(hbm, hbm, hbm),
        scratch_shapes=[
            vmem((256, 1024), f32),
            vmem((F, 8, 8, *tile), f32),
            *[vmem((BLOCKS, *tile), f32)] * 8,
            vmem((F, 8, SLOTS, *tile), f32),
            vmem((2, 8, SLOTS, *tile), f32),
            vmem((4, 8, 2, 4, *tile), f32),
            vmem((F, 8, SLOTS, *tile), f32),
            vmem((2, 8, SLOTS, *tile), f32),
            vmem((4, 8, 2, 4, *tile), f32),
            vmem((8, 16, 3, SLOTS), jnp.int32),
            pltpu.SMEM((8, 16, 3, SLOTS), jnp.int32),
            vmem(tile, f32),
            vmem((16, *tile), f32),
            vmem((BLOCKS, TILE), jnp.int32),
            vmem((256, 256), f32),
            vmem((TV, TILE, TILE), f32),
            vmem((128, BLOCKS * TILE), f32),
            vmem((8, SLOTS, F, *tile), f32),
            vmem((4, 8, 4, F, *tile), f32),
            vmem((BLOCKS, F, *tile), f32),
            dma((8,)), dma((8,)),
            dma((F, 8)), dma((F, 8)),
            dma((F,)), dma((F,)),
            dma((8,)), dma((8,)),
            dma((17,)), dma((16,)),
            dma((F, 8)), dma((F, 8)),
            dma((2, 8)), dma((2, 8)),
            dma((4, 8)), dma((4, 8)),
            dma((17,)),
        ],
        compiler_params=pltpu.CompilerParams(
            collective_id=0, has_side_effects=True, vmem_limit_bytes=56 * 2**20
        ),
    )(feat, deg, weight, lists, lists, hubs, tiles, hub_w)


def add_kernel(
    prod_own, prod_par, base, deg, bias, lists, counts,
    out,
    own_v, par_v, acc, deg_v, sem,
):
    get_base = pltpu.make_async_copy(base, acc, sem.at[0])
    get_own = pltpu.make_async_copy(prod_own, own_v, sem.at[1])
    get_par = pltpu.make_async_copy(prod_par, par_v, sem.at[2])
    get_deg = pltpu.make_async_copy(deg, deg_v, sem.at[3])
    copies = (get_base, get_own, get_par, get_deg)
    for copy in copies:
        copy.start()
    yh = lax.axis_index("blk") // 8
    nar = lax.axis_index("narrow")
    sub = lax.broadcasted_iota(jnp.int32, (8, TILE), 0)
    biases = []
    for f in range(F):
        column = jnp.zeros((8, TILE), jnp.float32)
        for i in range(8):
            column = jnp.where(sub == i, bias[nar * 32 + f * 8 + i], column)
        biases.append(column)
    for copy in copies:
        copy.wait()

    def own_source(i, carry):
        o = yh * 8 + i

        def slot(k, carry):
            r = lists[0, o, 0, k]
            acc[r] += own_v[i, k]
            return carry

        return lax.fori_loop(0, counts[0, o], slot, carry)

    def par_source(i, carry):
        o = (1 - yh) * 8 + i

        def slot(k, carry):
            r = lists[0, o, 0, k]
            acc[r] += par_v[k // 4, i, lax.rem(k, 4)]
            return carry

        return lax.fori_loop(0, counts[0, o], slot, carry)

    lax.fori_loop(0, 8, own_source, 0)
    lax.fori_loop(0, 8, par_source, 0)

    def finish(i, carry):
        inv = lax.rsqrt(deg_v[pl.ds(pl.multiple_of(i * 8, 8), 8), :].astype(jnp.float32))
        for b in range(8):
            for f in range(F):
                value = acc[i * 8 + b, f] * inv[b : b + 1, :] + biases[f]
                out[f * 8 : f * 8 + 8, pl.ds(pl.multiple_of((i * 8 + b) * TILE, TILE), TILE)] = (
                    jnp.maximum(value, 0.0)
                )
        return carry

    lax.fori_loop(0, 8, finish, 0)


def add_rows(prod_own, prod_par, base, deg, bias, lists, counts):
    f32 = jnp.float32
    vmem = pltpu.VMEM
    smem = pl.BlockSpec(memory_space=pltpu.SMEM)
    hbm = pl.BlockSpec(memory_space=pl.ANY)
    tile = (8, TILE)
    return pl.pallas_call(
        add_kernel,
        out_shape=jax.ShapeDtypeStruct((32, BLOCKS * TILE), f32),
        in_specs=[hbm, hbm, hbm, hbm, smem, smem, smem],
        out_specs=pl.BlockSpec(memory_space=vmem),
        scratch_shapes=[
            vmem((8, SLOTS, F, *tile), f32),
            vmem((4, 8, 4, F, *tile), f32),
            vmem((BLOCKS, F, *tile), f32),
            vmem((BLOCKS, TILE), jnp.int32),
            pltpu.SemaphoreType.DMA((4,)),
        ],
        compiler_params=pltpu.CompilerParams(vmem_limit_bytes=24 * 2**20),
    )(prod_own, prod_par, base, deg, bias, lists, counts)


def body(
    features, degrees, tile_values, tile_list, tile_count, hub_local, hub_weights, weight, out_bias
):
    deg = degrees.reshape(BLOCKS, TILE)
    own, par, base = exchange(
        features, deg, weight, tile_list, hub_local, tile_values, hub_weights
    )
    return add_rows(own, par, base, deg, out_bias, tile_list, tile_count)


def solution(mesh):
    return jax.shard_map(
        body,
        mesh=mesh,
        in_specs=(
            P("narrow", "blk"),
            P("blk"),
            P("blk", None, None),
            P("blk", None, None, None),
            P("blk", None),
            P("blk", None),
            P(None, "blk"),
            P(),
            P(),
        ),
        out_specs=P("narrow", "blk"),
        check_vma=False,
    )
```

```python
import functools

import jax
import jax.numpy as jnp
from jax import lax
from jax.experimental import pallas as pl
from jax.experimental.pallas import tpu as pltpu
from jax.sharding import PartitionSpec as P

TILE = 128
SLOTS = 16
F = 4
BLOCKS = 64
TV = 256
MESH = pl.DeviceIdType.MESH
ROW = ((1, 0), (3, 0), (1, 1), (3, 1), (2, 0), (2, 1), (0, 1))
NARROW = ((1, 0), (3, 0), (0, 1), (2, 0), (1, 1), (3, 1), (2, 1))


def split(x):
    hi = x.astype(jnp.bfloat16)
    lo = (x - hi.astype(jnp.float32)).astype(jnp.bfloat16)
    return hi, lo


def nt_dot(a, b):
    return lax.dot_general(a, b, (((1,), (1,)), ((), ())), preferred_element_type=jnp.float32)


def nn_dot(a, b):
    return jnp.dot(a, b, preferred_element_type=jnp.float32)


def exchange_kernel(
    feat, deg, weight, lists, my_list, counts, hubs, tiles, hub_w,
    out,
    xt, ysend, ya, yb, yc, yd, pa, pb, pc, pd, own_b, early_b, late_b,
    got_own, got_early, got_late, lists_v, lists_s, hub_v, hub_in, deg_v, w_v, raw_t, t_v, hw_v,
    order_v, order_s, value,
    s1, r1, s2, r2, sy, ry, sl, rl, sh, rh, so, ro, se, re, sq, rq, loc,
):
    y4, yp = (ya, yb, yc, yd), (pa, pb, pc, pd)
    blk = lax.axis_index("blk")
    nar = lax.axis_index("narrow")
    yh, x, core = blk // 8, (blk // 2) % 4, blk % 2
    z, yl = nar // 2, nar % 2
    me = x * 2 + core
    partner = (1 - yh) * 8 + me

    def row_peer(step, other):
        return lax.rem(x + step, 4) * 2 + lax.rem(core + other, 2)

    def narrow_peer(step, other):
        return lax.rem(z + step, 4) * 2 + lax.rem(yl + other, 2)

    bar = pltpu.get_barrier_semaphore()
    for step, other in NARROW:
        pl.semaphore_signal(
            bar, inc=1, device_id=(blk, narrow_peer(step, other)), device_id_type=MESH
        )
    for step, other in ROW:
        pl.semaphore_signal(
            bar, inc=1, device_id=(yh * 8 + row_peer(step, other), nar), device_id_type=MESH
        )
    pl.semaphore_signal(bar, inc=1, device_id=(partner, nar), device_id_type=MESH)

    get_deg = pltpu.make_async_copy(deg, deg_v, loc.at[0])
    get_w = pltpu.make_async_copy(weight, w_v, loc.at[1])
    get_own = pltpu.make_async_copy(
        feat.at[:, pl.ds(pl.multiple_of(nar * 1024, 1024), 1024)],
        xt.at[pl.ds(pl.multiple_of(nar * 32, 32), 32), :], loc.at[2],
    )
    get_list = pltpu.make_async_copy(lists.at[0, 1], lists_v.at[0], loc.at[3])
    def get_t(part):
        return pltpu.make_async_copy(
            tiles.at[pl.ds(part * 64, 64)], raw_t.at[part % 2], loc.at[11 + part]
        )

    get_hw = pltpu.make_async_copy(hub_w, hw_v, loc.at[5])
    for copy in (get_w, get_deg, get_own, get_list):
        copy.start()
    pl.semaphore_wait(bar, 15)

    def send1(n, to):
        return pltpu.make_async_remote_copy(
            src_ref=feat.at[:, pl.ds(pl.multiple_of(to * 1024, 1024), 1024)],
            dst_ref=xt.at[pl.ds(pl.multiple_of(n * 32, 32), 32), :],
            send_sem=s1.at[to], recv_sem=r1.at[n],
            device_id=(blk, to), device_id_type=MESH,
        )

    for step, other in NARROW:
        send1(nar, narrow_peer(step, other)).start()

    def send_list(step, other):
        slot = step * 2 + other
        return pltpu.make_async_remote_copy(
            src_ref=lists.at[0, 1], dst_ref=lists_v.at[slot],
            send_sem=sl.at[slot], recv_sem=rl.at[slot],
            device_id=(yh * 8 + row_peer(4 - step, other), nar), device_id_type=MESH,
        )

    for step, other in ROW:
        send_list(step, other).start()
    get_t(0).start()
    get_t(1).start()
    get_hw.start()

    get_w.wait()
    get_deg.wait()
    wh, wl = split(w_v[...].T)
    inv = lax.rsqrt(deg_v[pl.ds(pl.multiple_of(nar * 8, 8), 8), :].astype(jnp.float32))

    position = lax.broadcasted_iota(jnp.int32, (8, TILE), 0) * TILE + lax.broadcasted_iota(
        jnp.int32, (8, TILE), 1
    )

    def slot_at(s):
        late = s - 128
        own = s < 128
        i = jnp.where(own, s // 16, late % 32 // 4)
        k = jnp.where(own, s % 16, late // 32 * 4 + late % 4)
        o = jnp.where(own, yh, 1 - yh) * 8 + i
        return my_list[0, 0, o, k], k < counts[0, o]

    def fill(s, rows):
        r, live = slot_at(s)
        return jnp.where(position == s, jnp.where(live, r, 2000 + r), rows)

    rows = lax.fori_loop(0, TV, fill, jnp.zeros((8, TILE), jnp.int32))

    def link(s, carry):
        before, last = carry
        r, live = slot_at(s)
        r = jnp.where(live, r, 1000)
        before = jnp.where((rows == r) & (position > s), BLOCKS + s, before)
        return before, jnp.where(position == r, BLOCKS + s, last)

    before, last = lax.fori_loop(0, TV, link, (jnp.where(rows >= 2000, 0, rows), position))
    order_v[:8] = before
    order_v[8:] = last
    order_to_smem = pltpu.make_async_copy(order_v, order_s, loc.at[15])
    order_to_smem.start()

    for part in range(4):
        get_t(part).wait()

        def halves(t, carry, part=part):
            hi, lo = split(raw_t[part % 2, t])
            t_v[part * 64 + t, :, :TILE] = hi
            t_v[part * 64 + t, :, TILE:] = lo
            return carry

        lax.fori_loop(0, 64, halves, 0)
        if part < 2:
            get_t(part + 2).start()
    order_to_smem.wait()

    get_own.wait()
    for step, other in NARROW:
        n = narrow_peer(step, other)
        send1(n, n).wait_recv()

    for b in range(8):
        xh, xl = split(xt[:, b * TILE : (b + 1) * TILE])
        y = nn_dot(wh, xh) + nn_dot(wl, xh) + nn_dot(wh, xl)
        y = y * inv[b : b + 1, :]
        for n in range(8):
            for f in range(F):
                row = n * 32 + f * 8
                ysend[f, n, b] = y[row : row + 8, :]

    def send2(f, n, to):
        return pltpu.make_async_remote_copy(
            src_ref=ysend.at[f, to],
            dst_ref=y4[f].at[pl.ds(pl.multiple_of(n * 8, 8), 8)],
            send_sem=s2.at[f, to], recv_sem=r2.at[f, n],
            device_id=(blk, to), device_id_type=MESH,
        )

    def own2(f):
        return pltpu.make_async_copy(
            ysend.at[f, nar], y4[f].at[pl.ds(pl.multiple_of(nar * 8, 8), 8)], loc.at[6 + f]
        )

    for f in range(F):
        for step, other in NARROW:
            send2(f, nar, narrow_peer(step, other)).start()
        own2(f).start()

    get_list.wait()
    for step, other in ROW:
        send_list(step, other).wait_recv()
    to_smem = pltpu.make_async_copy(lists_v, lists_s, loc.at[10])
    to_smem.start()
    to_smem.wait()

    def send_y(f):
        return pltpu.make_async_remote_copy(
            src_ref=y4[f], dst_ref=yp[f], send_sem=sy.at[f], recv_sem=ry.at[f],
            device_id=(partner, nar), device_id_type=MESH,
        )

    def send_blocks(buf, got, ssem, rsem, part, source, step, other):
        slot = step * 2 + other
        return pltpu.make_async_remote_copy(
            src_ref=buf.at[part, slot], dst_ref=got.at[part, source],
            send_sem=ssem.at[part, slot], recv_sem=rsem.at[part, source],
            device_id=(yh * 8 + row_peer(step, other), nar), device_id_type=MESH,
        )

    def column(slot, source, k):
        return lists_s[slot, source, k]

    def send_own(f, source, step, other):
        return send_blocks(own_b, got_own, so, ro, f, source, step, other)

    def send_early(f, source, step, other):
        return send_blocks(early_b, got_early, se, re, f, source, step, other)

    def send_late(q, source, step, other):
        return send_blocks(late_b, got_late, sq, rq, q, source, step, other)

    for f in range(F):
        own2(f).wait()
        for step, other in NARROW:
            n = narrow_peer(step, other)
            send2(f, n, n).wait_recv()
        send_y(f).start()
        for step, other in ROW:
            slot = step * 2 + other
            for k in range(SLOTS):
                own_b[f, slot, k] = y4[f][column(slot, blk, k)]
            send_own(f, me, step, other).start()
        for k in range(SLOTS):
            got_own[f, me, k] = y4[f][column(0, blk, k)]

    lane = lax.broadcasted_iota(jnp.int32, (8, TILE), 1)
    hub = jnp.zeros((8, TILE), jnp.float32)
    for h in range(8):
        node = hubs[0, h]
        here = lane == lax.rem(node, TILE)
        for f in range(F):
            col = jnp.sum(jnp.where(here, y4[f][node // TILE], 0.0), axis=1, keepdims=True)
            hub = jnp.where(lane == f * 8 + h, col, hub)
    hub_v[...] = hub
    hub_in[blk] = hub

    def swap_hub(source):
        return pltpu.make_async_remote_copy(
            src_ref=hub_v, dst_ref=hub_in.at[source], send_sem=sh.at[16], recv_sem=rh.at[source],
            device_id=(partner, nar), device_id_type=MESH,
        )

    def send_hub(src, source, sem, step, other):
        return pltpu.make_async_remote_copy(
            src_ref=src, dst_ref=hub_in.at[source], send_sem=sh.at[sem],
            recv_sem=rh.at[source],
            device_id=(yh * 8 + row_peer(step, other), nar), device_id_type=MESH,
        )

    swap_hub(blk).start()
    for step, other in ROW:
        send_hub(hub_v, blk, step * 2 + other, step, other).start()

    def own_left(f):
        for step, other in ROW:
            send_own(f, me, step, other).wait_send()

    for f in range(2):
        send_y(f).wait_recv()
        own_left(f)
        for step, other in ROW:
            slot = step * 2 + other
            for k in range(SLOTS):
                early_b[f, slot, k] = yp[f][column(slot, partner, k)]
            send_early(f, me, step, other).start()
        for k in range(SLOTS):
            got_early[f, me, k] = yp[f][column(0, partner, k)]

    swap_hub(partner).wait_recv()
    for step, other in ROW:
        send_hub(hub_in.at[partner], partner, 8 + step * 2 + other, step, other).start()

    own_left(2)
    own_left(3)
    for f in range(F):
        send_y(f).wait_send()
        for step, other in NARROW:
            n = narrow_peer(step, other)
            send2(f, n, n).wait_send()
    for step, other in NARROW:
        n = narrow_peer(step, other)
        send1(n, n).wait_send()
    for step, other in ROW:
        send_list(step, other).wait_send()

    for step, other in ROW:
        peer = row_peer(step, other)
        for o in (yh * 8 + peer, (1 - yh) * 8 + peer):
            send_hub(hub_v, o, 0, step, other).wait_recv()
    parts = []
    for f in range(F):
        total = jnp.zeros((8, TILE), jnp.float32)
        for o in range(16):
            moved = pltpu.roll(hub_in[o], (o * 8 - f * 8) % TILE, 1)
            total = jnp.where(lane // 8 == o, moved, total)
        parts.append(total)
    gh, gl = split(jnp.concatenate(parts, axis=0))
    g2 = jnp.concatenate([gh, gl], axis=0)
    get_hw.wait()

    def hub_sum(i, carry):
        hh, hl = split(hw_v[:, pl.ds(pl.multiple_of(i * 512, 512), 512)])
        p = nn_dot(g2, hh)
        p = p[:32] + p[32:] + nn_dot(gh, hl)
        for b in range(4):
            for f in range(F):
                value[i * 4 + b, f] = (
                    p[f * 8 : f * 8 + 8, b * TILE : (b + 1) * TILE] + y4[f][i * 4 + b]
                )
        return carry

    lax.fori_loop(0, 16, hub_sum, 0)

    def product(xs, t):
        xh, xl = split(xs)
        x2 = jnp.concatenate(
            [
                jnp.concatenate([xh, xh], axis=1),
                jnp.concatenate([xl, jnp.zeros_like(xl)], axis=1),
            ],
            axis=0,
        )
        p = nt_dot(x2, t_v[t])
        return p[:32] + p[32:]

    def add(products, first):
        for j, p in enumerate(products):
            s = first + j
            back = order_s[s // TILE, lax.rem(s, TILE)]
            for f in range(F):
                value[BLOCKS + s, f] = p[f * 8 : f * 8 + 8, :] + value[back, f]

    def own_products(i, carry):
        for half in range(2):
            products = []
            for k in range(half * 8, half * 8 + 8):
                xs = jnp.concatenate([got_own[f, i, k] for f in range(F)], axis=0)
                products.append(product(xs, my_list[0, 2, yh * 8 + i, k]))
            add(products, i * 16 + half * 8)
        return carry

    def par_products(q):
        def pair(i, carry):
            products = []
            for j in range(2):
                for k in range(4):
                    xs = jnp.concatenate(
                        [got_early[f, i * 2 + j, q * 4 + k] for f in range(2)]
                        + [got_late[q, i * 2 + j, f, k] for f in range(2)],
                        axis=0,
                    )
                    t = my_list[0, 2, (1 - yh) * 8 + i * 2 + j, q * 4 + k]
                    products.append(product(xs, t))
            add(products, 128 + q * 32 + i * 8)
            return carry

        lax.fori_loop(0, 4, pair, 0)

    for f in range(2, F):
        send_y(f).wait_recv()

    def start_late(q):
        for step, other in ROW:
            slot = step * 2 + other
            for k in range(4):
                c = column(slot, partner, q * 4 + k)
                for f in range(2):
                    late_b[q, slot, f, k] = yp[2 + f][c]
            send_late(q, me, step, other).start()
        for k in range(4):
            c = column(0, partner, q * 4 + k)
            for f in range(2):
                got_late[q, me, f, k] = yp[2 + f][c]

    def late_done(q):
        for step, other in ROW:
            send_late(q, row_peer(step, other), step, other).wait()

    start_late(0)
    start_late(1)
    for f in range(F):
        for step, other in ROW:
            send_own(f, row_peer(step, other), step, other).wait_recv()
    lax.fori_loop(0, 8, own_products, 0)
    swap_hub(partner).wait_send()
    for step, other in ROW:
        send_hub(hub_v, blk, step * 2 + other, step, other).wait_send()
        send_hub(hub_v, blk, 8 + step * 2 + other, step, other).wait_send()
    for f in range(2):
        for step, other in ROW:
            send_early(f, row_peer(step, other), step, other).wait()
    for q in range(4):
        late_done(q)
        if q < 2:
            start_late(q + 2)
        par_products(q)

    def finish(i, carry):
        inv = lax.rsqrt(deg_v[pl.ds(pl.multiple_of(i * 8, 8), 8), :].astype(jnp.float32))
        for b in range(8):
            end = order_s[8, i * 8 + b]
            for f in range(F):
                out[f * 8 : f * 8 + 8, pl.ds(pl.multiple_of((i * 8 + b) * TILE, TILE), TILE)] = (
                    value[end, f] * inv[b : b + 1, :]
                )
        return carry

    lax.fori_loop(0, 8, finish, 0)


def exchange(feat, deg, weight, lists, counts, hubs, tiles, hub_w):
    f32, bf16 = jnp.float32, jnp.bfloat16
    dma = pltpu.SemaphoreType.DMA
    vmem = pltpu.VMEM
    smem = pl.BlockSpec(memory_space=pltpu.SMEM)
    hbm = pl.BlockSpec(memory_space=pl.ANY)
    tile = (8, TILE)
    return pl.pallas_call(
        exchange_kernel,
        out_shape=jax.ShapeDtypeStruct((32, BLOCKS * TILE), f32),
        in_specs=[hbm, hbm, hbm, hbm, smem, smem, smem, hbm, hbm],
        out_specs=pl.BlockSpec(memory_space=vmem),
        scratch_shapes=[
            vmem((256, 1024), f32),
            vmem((F, 8, 8, *tile), f32),
            *[vmem((BLOCKS, *tile), f32)] * 8,
            vmem((F, 8, SLOTS, *tile), f32),
            vmem((2, 8, SLOTS, *tile), f32),
            vmem((4, 8, 2, 4, *tile), f32),
            vmem((F, 8, SLOTS, *tile), f32),
            vmem((2, 8, SLOTS, *tile), f32),
            vmem((4, 8, 2, 4, *tile), f32),
            vmem((8, 16, SLOTS), jnp.int32),
            pltpu.SMEM((8, 16, SLOTS), jnp.int32),
            vmem(tile, f32),
            vmem((16, *tile), f32),
            vmem((BLOCKS, TILE), jnp.int32),
            vmem((256, 256), f32),
            vmem((2, 64, TILE, TILE), f32),
            vmem((TV, TILE, 2 * TILE), bf16),
            vmem((128, BLOCKS * TILE), f32),
            vmem((16, TILE), jnp.int32),
            pltpu.SMEM((16, TILE), jnp.int32),
            vmem((BLOCKS + TV, F, *tile), f32),
            dma((8,)), dma((8,)),
            dma((F, 8)), dma((F, 8)),
            dma((F,)), dma((F,)),
            dma((8,)), dma((8,)),
            dma((17,)), dma((16,)),
            dma((F, 8)), dma((F, 8)),
            dma((2, 8)), dma((2, 8)),
            dma((4, 8)), dma((4, 8)),
            dma((16,)),
        ],
        compiler_params=pltpu.CompilerParams(
            collective_id=0, has_side_effects=True, vmem_limit_bytes=60 * 2**20
        ),
    )(feat, deg, weight, lists, lists, counts, hubs, tiles, hub_w)


def body(
    features, degrees, tile_values, tile_list, tile_count, hub_local, hub_weights, weight, out_bias
):
    deg = degrees.reshape(BLOCKS, TILE)
    lists = jnp.transpose(tile_list, (0, 2, 1, 3))
    aggregated = exchange(
        features, deg, weight, lists, tile_count, hub_local, tile_values, hub_weights
    )
    bias = lax.dynamic_slice_in_dim(out_bias, lax.axis_index("narrow") * 32, 32)
    return jnp.maximum(aggregated + bias[:, None], 0.0)


def solution(mesh):
    return jax.shard_map(
        body,
        mesh=mesh,
        in_specs=(
            P("narrow", "blk"),
            P("blk"),
            P("blk", None, None),
            P("blk", None, None, None),
            P("blk", None),
            P("blk", None),
            P(None, "blk"),
            P(),
            P(),
        ),
        out_specs=P("narrow", "blk"),
        check_vma=False,
    )
```

```python
import functools

import jax
import jax.numpy as jnp
from jax import lax
from jax.experimental import pallas as pl
from jax.experimental.pallas import tpu as pltpu
from jax.sharding import PartitionSpec as P

TILE = 128
SLOTS = 16
F = 4
BLOCKS = 64
TV = 256
MESH = pl.DeviceIdType.MESH
ROW = ((1, 0), (3, 0), (1, 1), (3, 1), (2, 0), (2, 1), (0, 1))
NARROW = ((1, 0), (3, 0), (0, 1), (2, 0), (1, 1), (3, 1), (2, 1))


def split(x):
    hi = x.astype(jnp.bfloat16)
    lo = (x - hi.astype(jnp.float32)).astype(jnp.bfloat16)
    return hi, lo


def nt_dot(a, b):
    return lax.dot_general(a, b, (((1,), (1,)), ((), ())), preferred_element_type=jnp.float32)


def nn_dot(a, b):
    return jnp.dot(a, b, preferred_element_type=jnp.float32)


def exchange_kernel(
    feat, deg, weight, lists, my_list, counts, hubs, bias, tiles, hub_w,
    out,
    xt, ysend, ya, yb, yc, yd, pa, pb, pc, pd, own_b, early_b, late_b,
    got_own, got_early, got_late, lists_v, lists_s, hub_v, hub_in, deg_v, w_v, raw_t, t_v, hw_v,
    order_v, order_s, value, hub_sums,
    s1, r1, s2, r2, sy, ry, sl, rl, sh, rh, so, ro, se, re, sq, rq, loc,
):
    y4, yp = (ya, yb, yc, yd), (pa, pb, pc, pd)
    blk = lax.axis_index("blk")
    nar = lax.axis_index("narrow")
    yh, x, core = blk // 8, (blk // 2) % 4, blk % 2
    z, yl = nar // 2, nar % 2
    me = x * 2 + core
    partner = (1 - yh) * 8 + me

    def row_peer(step, other):
        return lax.rem(x + step, 4) * 2 + lax.rem(core + other, 2)

    def narrow_peer(step, other):
        return lax.rem(z + step, 4) * 2 + lax.rem(yl + other, 2)

    bar = pltpu.get_barrier_semaphore()
    for step, other in NARROW:
        pl.semaphore_signal(
            bar, inc=1, device_id=(blk, narrow_peer(step, other)), device_id_type=MESH
        )
    for step, other in ROW:
        pl.semaphore_signal(
            bar, inc=1, device_id=(yh * 8 + row_peer(step, other), nar), device_id_type=MESH
        )
    pl.semaphore_signal(bar, inc=1, device_id=(partner, nar), device_id_type=MESH)

    get_deg = pltpu.make_async_copy(deg, deg_v, loc.at[0])
    get_w = pltpu.make_async_copy(weight, w_v, loc.at[1])
    get_own = pltpu.make_async_copy(
        feat.at[:, pl.ds(pl.multiple_of(nar * 1024, 1024), 1024)],
        xt.at[pl.ds(pl.multiple_of(nar * 32, 32), 32), :], loc.at[2],
    )
    get_list = pltpu.make_async_copy(lists.at[0, 1], lists_v.at[0], loc.at[3])
    def get_t(part):
        return pltpu.make_async_copy(
            tiles.at[pl.ds(part * 64, 64)], raw_t.at[part % 2], loc.at[11 + part]
        )

    get_hw = pltpu.make_async_copy(hub_w, hw_v, loc.at[5])
    for copy in (get_w, get_deg, get_own, get_list):
        copy.start()
    pl.semaphore_wait(bar, 15)

    def send1(n, to):
        return pltpu.make_async_remote_copy(
            src_ref=feat.at[:, pl.ds(pl.multiple_of(to * 1024, 1024), 1024)],
            dst_ref=xt.at[pl.ds(pl.multiple_of(n * 32, 32), 32), :],
            send_sem=s1.at[to], recv_sem=r1.at[n],
            device_id=(blk, to), device_id_type=MESH,
        )

    for step, other in NARROW:
        send1(nar, narrow_peer(step, other)).start()

    def send_list(step, other):
        slot = step * 2 + other
        return pltpu.make_async_remote_copy(
            src_ref=lists.at[0, 1], dst_ref=lists_v.at[slot],
            send_sem=sl.at[slot], recv_sem=rl.at[slot],
            device_id=(yh * 8 + row_peer(4 - step, other), nar), device_id_type=MESH,
        )

    for step, other in ROW:
        send_list(step, other).start()
    get_t(0).start()
    get_t(1).start()
    get_hw.start()

    get_w.wait()
    get_deg.wait()
    wh, wl = split(w_v[...].T)
    inv = lax.rsqrt(deg_v[pl.ds(pl.multiple_of(nar * 8, 8), 8), :].astype(jnp.float32))

    position = lax.broadcasted_iota(jnp.int32, (8, TILE), 0) * TILE + lax.broadcasted_iota(
        jnp.int32, (8, TILE), 1
    )

    def key(o, k, dead):
        r = my_list[0, 0, o, k]
        return jnp.where(k < counts[0, o], r, dead + r)

    def fill_own(i, rows):
        for k in range(SLOTS):
            rows = jnp.where(position == i * 16 + k, key(yh * 8 + i, k, 2000), rows)
        return rows

    def fill_par(i, rows):
        for k in range(SLOTS):
            s = 128 + k // 4 * 32 + i * 4 + k % 4
            rows = jnp.where(position == s, key((1 - yh) * 8 + i, k, 2000), rows)
        return rows

    rows = lax.fori_loop(0, 8, fill_own, jnp.zeros((8, TILE), jnp.int32))
    rows = lax.fori_loop(0, 8, fill_par, rows)

    def link(r, s, carry):
        before, last = carry
        before = jnp.where((rows == r) & (position > s), BLOCKS + s, before)
        return before, jnp.where(position == r, BLOCKS + s, last)

    def link_own(i, carry):
        for k in range(SLOTS):
            carry = link(key(yh * 8 + i, k, 1000), i * 16 + k, carry)
        return carry

    def link_par(i, carry):
        for k in range(SLOTS):
            o = (1 - yh) * 8 + lax.rem(i, 2) * 4 + k // 4
            s = 128 + i * 16 + k
            carry = link(key(o, i // 2 * 4 + k % 4, 1000), s, carry)
        return carry

    carry = jnp.where(rows >= 2000, 0, rows), position
    carry = lax.fori_loop(0, 8, link_own, carry)
    before, last = lax.fori_loop(0, 8, link_par, carry)
    order_v[:8] = before
    order_v[8:] = last
    order_to_smem = pltpu.make_async_copy(order_v, order_s, loc.at[15])
    order_to_smem.start()

    for part in range(4):
        get_t(part).wait()

        def halves(t, carry, part=part):
            hi, lo = split(raw_t[part % 2, t])
            t_v[part * 64 + t, :, :TILE] = hi
            t_v[part * 64 + t, :, TILE:] = lo
            return carry

        lax.fori_loop(0, 64, halves, 0)
        if part < 2:
            get_t(part + 2).start()
    order_to_smem.wait()

    get_own.wait()
    for step, other in NARROW:
        n = narrow_peer(step, other)
        send1(n, n).wait_recv()

    for b in range(8):
        xh, xl = split(xt[:, b * TILE : (b + 1) * TILE])
        y = nn_dot(wh, xh) + nn_dot(wl, xh) + nn_dot(wh, xl)
        y = y * inv[b : b + 1, :]
        for n in range(8):
            for f in range(F):
                row = n * 32 + f * 8
                ysend[f, n, b] = y[row : row + 8, :]

    def send2(f, n, to):
        return pltpu.make_async_remote_copy(
            src_ref=ysend.at[f, to],
            dst_ref=y4[f].at[pl.ds(pl.multiple_of(n * 8, 8), 8)],
            send_sem=s2.at[f, to], recv_sem=r2.at[f, n],
            device_id=(blk, to), device_id_type=MESH,
        )

    def own2(f):
        return pltpu.make_async_copy(
            ysend.at[f, nar], y4[f].at[pl.ds(pl.multiple_of(nar * 8, 8), 8)], loc.at[6 + f]
        )

    for f in range(F):
        for step, other in NARROW:
            send2(f, nar, narrow_peer(step, other)).start()
        own2(f).start()

    get_list.wait()
    for step, other in ROW:
        send_list(step, other).wait_recv()
    to_smem = pltpu.make_async_copy(lists_v, lists_s, loc.at[10])
    to_smem.start()
    to_smem.wait()

    def send_y(f):
        return pltpu.make_async_remote_copy(
            src_ref=y4[f], dst_ref=yp[f], send_sem=sy.at[f], recv_sem=ry.at[f],
            device_id=(partner, nar), device_id_type=MESH,
        )

    def send_blocks(buf, got, ssem, rsem, part, source, step, other):
        slot = step * 2 + other
        return pltpu.make_async_remote_copy(
            src_ref=buf.at[part, slot], dst_ref=got.at[part, source],
            send_sem=ssem.at[part, slot], recv_sem=rsem.at[part, source],
            device_id=(yh * 8 + row_peer(step, other), nar), device_id_type=MESH,
        )

    def column(slot, source, k):
        return lists_s[slot, source, k]

    def send_own(f, source, step, other):
        return send_blocks(own_b, got_own, so, ro, f, source, step, other)

    def send_early(f, source, step, other):
        return send_blocks(early_b, got_early, se, re, f, source, step, other)

    def send_late(q, source, step, other):
        return send_blocks(late_b, got_late, sq, rq, q, source, step, other)

    lane = lax.broadcasted_iota(jnp.int32, (8, TILE), 1)

    def swap_hub(source):
        return pltpu.make_async_remote_copy(
            src_ref=hub_v, dst_ref=hub_in.at[source], send_sem=sh.at[16], recv_sem=rh.at[source],
            device_id=(partner, nar), device_id_type=MESH,
        )

    def send_hub(src, source, sem, step, other):
        return pltpu.make_async_remote_copy(
            src_ref=src, dst_ref=hub_in.at[source], send_sem=sh.at[sem],
            recv_sem=rh.at[source],
            device_id=(yh * 8 + row_peer(step, other), nar), device_id_type=MESH,
        )

    for f in range(F):
        own2(f).wait()
        for step, other in NARROW:
            n = narrow_peer(step, other)
            send2(f, n, n).wait_recv()
        if f == F - 1:
            hub = jnp.zeros((8, TILE), jnp.float32)
            for h in range(8):
                node = hubs[0, h]
                here = lane == lax.rem(node, TILE)
                for g in range(F):
                    col = jnp.sum(jnp.where(here, y4[g][node // TILE], 0.0), axis=1, keepdims=True)
                    hub = jnp.where(lane == g * 8 + h, col, hub)
            hub_v[...] = hub
            hub_in[blk] = hub
            swap_hub(blk).start()
            for step, other in ROW:
                send_hub(hub_v, blk, step * 2 + other, step, other).start()
        send_y(f).start()
        for step, other in ROW:
            slot = step * 2 + other
            for k in range(SLOTS):
                own_b[f, slot, k] = y4[f][column(slot, blk, k)]
            send_own(f, me, step, other).start()
        for k in range(SLOTS):
            got_own[f, me, k] = y4[f][column(0, blk, k)]

    def keep_y(b, carry):
        for f in range(F):
            value[b, f] = y4[f][b]
        return carry

    for f in range(2):
        send_y(f).wait_recv()
        for step, other in ROW:
            slot = step * 2 + other
            for k in range(SLOTS):
                early_b[f, slot, k] = yp[f][column(slot, partner, k)]
            send_early(f, me, step, other).start()
        for k in range(SLOTS):
            got_early[f, me, k] = yp[f][column(0, partner, k)]

    lax.fori_loop(0, BLOCKS, keep_y, 0)
    swap_hub(partner).wait_recv()
    for step, other in ROW:
        send_hub(hub_in.at[partner], partner, 8 + step * 2 + other, step, other).start()

    def product(xs, t):
        xh, xl = split(xs)
        x2 = jnp.concatenate(
            [
                jnp.concatenate([xh, xh], axis=1),
                jnp.concatenate([xl, jnp.zeros_like(xl)], axis=1),
            ],
            axis=0,
        )
        p = nt_dot(x2, t_v[t])
        return p[:32] + p[32:]

    def add(products, first):
        for j, p in enumerate(products):
            s = first + j
            back = order_s[s // TILE, lax.rem(s, TILE)]
            for f in range(F):
                value[BLOCKS + s, f] = p[f * 8 : f * 8 + 8, :] + value[back, f]

    def own_products(i, carry):
        for half in range(2):
            products = []
            for k in range(half * 8, half * 8 + 8):
                xs = jnp.concatenate([got_own[f, i, k] for f in range(F)], axis=0)
                products.append(product(xs, my_list[0, 2, yh * 8 + i, k]))
            add(products, i * 16 + half * 8)
        return carry

    def par_products(q):
        def pair(i, carry):
            products = []
            for j in range(2):
                for k in range(4):
                    xs = jnp.concatenate(
                        [got_early[f, i * 2 + j, q * 4 + k] for f in range(2)]
                        + [got_late[q, i * 2 + j, f, k] for f in range(2)],
                        axis=0,
                    )
                    t = my_list[0, 2, (1 - yh) * 8 + i * 2 + j, q * 4 + k]
                    products.append(product(xs, t))
            add(products, 128 + q * 32 + i * 8)
            return carry

        lax.fori_loop(0, 4, pair, 0)

    for f in range(2, F):
        send_y(f).wait_recv()

    def start_late(q):
        for step, other in ROW:
            slot = step * 2 + other
            for k in range(4):
                c = column(slot, partner, q * 4 + k)
                for f in range(2):
                    late_b[q, slot, f, k] = yp[2 + f][c]
            send_late(q, me, step, other).start()
        for k in range(4):
            c = column(0, partner, q * 4 + k)
            for f in range(2):
                got_late[q, me, f, k] = yp[2 + f][c]

    def late_done(q):
        for step, other in ROW:
            send_late(q, row_peer(step, other), step, other).wait()

    for q in range(4):
        start_late(q)
    for f in range(F):
        for step, other in ROW:
            send_own(f, row_peer(step, other), step, other).wait()
    lax.fori_loop(0, 8, own_products, 0)

    for step, other in ROW:
        peer = row_peer(step, other)
        for o in (yh * 8 + peer, (1 - yh) * 8 + peer):
            send_hub(hub_v, o, 0, step, other).wait_recv()
    parts = []
    for f in range(F):
        total = jnp.zeros((8, TILE), jnp.float32)
        for o in range(16):
            moved = pltpu.roll(hub_in[o], (o * 8 - f * 8) % TILE, 1)
            total = jnp.where(lane // 8 == o, moved, total)
        parts.append(total)
    gh, gl = split(jnp.concatenate(parts, axis=0))
    g2 = jnp.concatenate([gh, gl], axis=0)
    get_hw.wait()

    def hub_sum(i, carry):
        hh, hl = split(hw_v[:, pl.ds(pl.multiple_of(i * 512, 512), 512)])
        p = nn_dot(g2, hh)
        p = p[:32] + p[32:] + nn_dot(gh, hl)
        for b in range(4):
            for f in range(F):
                hub_sums[i * 4 + b, f] = p[f * 8 : f * 8 + 8, b * TILE : (b + 1) * TILE]
        return carry

    lax.fori_loop(0, 16, hub_sum, 0)

    for f in range(F):
        send_y(f).wait_send()
        for step, other in NARROW:
            n = narrow_peer(step, other)
            send2(f, n, n).wait_send()
    for step, other in NARROW:
        n = narrow_peer(step, other)
        send1(n, n).wait_send()
    for step, other in ROW:
        send_list(step, other).wait_send()
    swap_hub(partner).wait_send()
    for step, other in ROW:
        send_hub(hub_v, blk, step * 2 + other, step, other).wait_send()
        send_hub(hub_v, blk, 8 + step * 2 + other, step, other).wait_send()
    for f in range(2):
        for step, other in ROW:
            send_early(f, row_peer(step, other), step, other).wait()
    for q in range(4):
        late_done(q)
        par_products(q)

    sub = lax.broadcasted_iota(jnp.int32, (8, TILE), 0)
    biases = []
    for f in range(F):
        column_f = jnp.zeros((8, TILE), jnp.float32)
        for i in range(8):
            column_f = jnp.where(sub == i, bias[nar * 32 + f * 8 + i], column_f)
        biases.append(column_f)

    def finish(i, carry):
        inv = lax.rsqrt(deg_v[pl.ds(pl.multiple_of(i * 8, 8), 8), :].astype(jnp.float32))
        for b in range(8):
            end = order_s[8, i * 8 + b]
            for f in range(F):
                out[f * 8 : f * 8 + 8, pl.ds(pl.multiple_of((i * 8 + b) * TILE, TILE), TILE)] = (
                    jnp.maximum(
                        (value[end, f] + hub_sums[i * 8 + b, f]) * inv[b : b + 1, :] + biases[f],
                        0.0,
                    )
                )
        return carry

    lax.fori_loop(0, 8, finish, 0)


def exchange(feat, deg, weight, lists, counts, hubs, bias, tiles, hub_w):
    f32, bf16 = jnp.float32, jnp.bfloat16
    dma = pltpu.SemaphoreType.DMA
    vmem = pltpu.VMEM
    smem = pl.BlockSpec(memory_space=pltpu.SMEM)
    hbm = pl.BlockSpec(memory_space=pl.ANY)
    tile = (8, TILE)
    return pl.pallas_call(
        exchange_kernel,
        out_shape=jax.ShapeDtypeStruct((32, BLOCKS * TILE), f32),
        in_specs=[hbm, hbm, hbm, hbm, smem, smem, smem, smem, hbm, hbm],
        out_specs=pl.BlockSpec(memory_space=vmem),
        scratch_shapes=[
            vmem((256, 1024), f32),
            vmem((F, 8, 8, *tile), f32),
            *[vmem((BLOCKS, *tile), f32)] * 8,
            vmem((F, 8, SLOTS, *tile), f32),
            vmem((2, 8, SLOTS, *tile), f32),
            vmem((4, 8, 2, 4, *tile), f32),
            vmem((F, 8, SLOTS, *tile), f32),
            vmem((2, 8, SLOTS, *tile), f32),
            vmem((4, 8, 2, 4, *tile), f32),
            vmem((8, 16, SLOTS), jnp.int32),
            pltpu.SMEM((8, 16, SLOTS), jnp.int32),
            vmem(tile, f32),
            vmem((16, *tile), f32),
            vmem((BLOCKS, TILE), jnp.int32),
            vmem((256, 256), f32),
            vmem((2, 64, TILE, TILE), f32),
            vmem((TV, TILE, 2 * TILE), bf16),
            vmem((128, BLOCKS * TILE), f32),
            vmem((16, TILE), jnp.int32),
            pltpu.SMEM((16, TILE), jnp.int32),
            vmem((BLOCKS + TV, F, *tile), f32),
            vmem((BLOCKS, F, *tile), f32),
            dma((8,)), dma((8,)),
            dma((F, 8)), dma((F, 8)),
            dma((F,)), dma((F,)),
            dma((8,)), dma((8,)),
            dma((17,)), dma((16,)),
            dma((F, 8)), dma((F, 8)),
            dma((2, 8)), dma((2, 8)),
            dma((4, 8)), dma((4, 8)),
            dma((16,)),
        ],
        compiler_params=pltpu.CompilerParams(
            collective_id=0, has_side_effects=True, vmem_limit_bytes=60 * 2**20
        ),
    )(feat, deg, weight, lists, lists, counts, hubs, bias, tiles, hub_w)


def body(
    features, degrees, tile_values, tile_list, tile_count, hub_local, hub_weights, weight, out_bias
):
    deg = degrees.reshape(BLOCKS, TILE)
    lists = jnp.transpose(tile_list, (0, 2, 1, 3))
    return exchange(
        features, deg, weight, lists, tile_count, hub_local, out_bias, tile_values, hub_weights
    )


def solution(mesh):
    return jax.shard_map(
        body,
        mesh=mesh,
        in_specs=(
            P("narrow", "blk"),
            P("blk"),
            P("blk", None, None),
            P("blk", None, None, None),
            P("blk", None),
            P("blk", None),
            P(None, "blk"),
            P(),
            P(),
        ),
        out_specs=P("narrow", "blk"),
        check_vma=False,
    )
```

```python
import functools

import jax
import jax.numpy as jnp
from jax import lax
from jax.experimental import pallas as pl
from jax.experimental.pallas import tpu as pltpu
from jax.sharding import PartitionSpec as P

TILE = 128
SLOTS = 16
F = 4
BLOCKS = 64
TV = 256
LEVELS = ((0, 4), (4, 4), (8, 4), (12, 2), (14, 2))
MESH = pl.DeviceIdType.MESH
ROW = ((2, 0), (2, 1), (1, 0), (3, 0), (1, 1), (3, 1), (0, 1))
FAR = ((2, 1), (1, 1), (3, 1), (0, 1), (2, 0), (1, 0), (3, 0))
NARROW = ((1, 0), (3, 0), (0, 1), (2, 0), (1, 1), (3, 1), (2, 1))


def split(x):
    hi = x.astype(jnp.bfloat16)
    lo = (x - hi.astype(jnp.float32)).astype(jnp.bfloat16)
    return hi, lo


def nt_dot(a, b):
    return lax.dot_general(a, b, (((1,), (1,)), ((), ())), preferred_element_type=jnp.float32)


def nn_dot(a, b):
    return jnp.dot(a, b, preferred_element_type=jnp.float32)


def exchange_kernel(
    feat, deg, weight, lists, my_list, counts, hubs, bias, tiles, hub_w,
    out_hbm,
    xt, ysend, ya, yb, yc, yd, pb, pc, pd, own_b, early_b, late_b,
    row1, row2, row3, sel_b, got_first,
    got_own, got_early, got_late, lists_v, lists_s, hub_v, hub_in, deg_v, w_v, raw_t, t_v, hw_v,
    order_v, order_s, value, hub_sums, out,
    s1, r1, s2, r2, sy, ry, sl, rl, sh, rh, so, ro, se, re, sq, rq, sb, rb, sf, rf, loc,
):
    y4, yp = (ya, yb, yc, yd), (None, pb, pc, pd)
    blk = lax.axis_index("blk")
    nar = lax.axis_index("narrow")
    yh, x, core = blk // 8, (blk // 2) % 4, blk % 2
    z, yl = nar // 2, nar % 2
    me = x * 2 + core
    partner = (1 - yh) * 8 + me

    def row_peer(step, other):
        return lax.rem(x + step, 4) * 2 + lax.rem(core + other, 2)

    def narrow_peer(step, other):
        return lax.rem(z + step, 4) * 2 + lax.rem(yl + other, 2)

    bar = pltpu.get_barrier_semaphore()
    for step, other in NARROW:
        pl.semaphore_signal(
            bar, inc=1, device_id=(blk, narrow_peer(step, other)), device_id_type=MESH
        )
    for step, other in ROW:
        pl.semaphore_signal(
            bar, inc=1, device_id=(yh * 8 + row_peer(step, other), nar), device_id_type=MESH
        )
    chip = (None, blk - core + 1 - core, partner, partner - core + 1 - core)
    for to in chip[2:]:
        pl.semaphore_signal(bar, inc=1, device_id=(to, nar), device_id_type=MESH)

    get_deg = pltpu.make_async_copy(deg, deg_v, loc.at[0])
    get_w = pltpu.make_async_copy(weight, w_v, loc.at[1])
    get_own = pltpu.make_async_copy(
        feat.at[:, pl.ds(pl.multiple_of(nar * 1024, 1024), 1024)],
        xt.at[pl.ds(pl.multiple_of(nar * 32, 32), 32), :], loc.at[2],
    )
    get_list = pltpu.make_async_copy(lists.at[0, 1], lists_v.at[0], loc.at[3])
    def get_t(part):
        return pltpu.make_async_copy(
            tiles.at[pl.ds(part * 64, 64)], raw_t.at[part % 2], loc.at[11 + part]
        )

    get_hw = pltpu.make_async_copy(hub_w, hw_v, loc.at[5])
    for copy in (get_w, get_deg, get_own, get_list):
        copy.start()
    pl.semaphore_wait(bar, 16)

    def send1(n, to):
        return pltpu.make_async_remote_copy(
            src_ref=feat.at[:, pl.ds(pl.multiple_of(to * 1024, 1024), 1024)],
            dst_ref=xt.at[pl.ds(pl.multiple_of(n * 32, 32), 32), :],
            send_sem=s1.at[to], recv_sem=r1.at[n],
            device_id=(blk, to), device_id_type=MESH,
        )

    for step, other in FAR:
        send1(nar, narrow_peer(step, other)).start()

    def send_list(step, other):
        slot = step * 2 + other
        return pltpu.make_async_remote_copy(
            src_ref=lists.at[0, 1], dst_ref=lists_v.at[slot],
            send_sem=sl.at[slot], recv_sem=rl.at[slot],
            device_id=(yh * 8 + row_peer(4 - step, other), nar), device_id_type=MESH,
        )

    def list_across(g):
        return pltpu.make_async_remote_copy(
            src_ref=lists.at[0, 1], dst_ref=lists_v.at[6 + g],
            send_sem=sl.at[6 + g], recv_sem=rl.at[6 + g],
            device_id=(chip[g], nar), device_id_type=MESH,
        )

    for step, other in ROW:
        send_list(step, other).start()
    for g in (2, 3):
        list_across(g).start()
    get_t(0).start()
    get_t(1).start()
    get_hw.start()

    get_w.wait()
    get_deg.wait()
    inv = lax.rsqrt(deg_v[pl.ds(pl.multiple_of(nar * 8, 8), 8), :].astype(jnp.float32))

    position = lax.broadcasted_iota(jnp.int32, (8, TILE), 0) * TILE + lax.broadcasted_iota(
        jnp.int32, (8, TILE), 1
    )

    def key(o, k, dead):
        r = my_list[0, 0, o, k]
        return jnp.where(k < counts[0, o], r, dead + r)

    def fill_own(i, rows):
        for k in range(SLOTS):
            rows = jnp.where(position == i * 16 + k, key(yh * 8 + i, k, 2000), rows)
        return rows

    def fill_par(i, rows):
        for first, wide in LEVELS:
            for k in range(wide):
                s = 128 + first * 8 + i * wide + k
                rows = jnp.where(position == s, key((1 - yh) * 8 + i, first + k, 2000), rows)
        return rows

    rows = lax.fori_loop(0, 8, fill_own, jnp.zeros((8, TILE), jnp.int32))
    rows = lax.fori_loop(0, 8, fill_par, rows)

    def link(r, s, carry):
        before, last = carry
        before = jnp.where((rows == r) & (position > s), BLOCKS + s, before)
        return before, jnp.where(position == r, BLOCKS + s, last)

    def link_own(i, carry):
        for k in range(SLOTS):
            carry = link(key(yh * 8 + i, k, 1000), i * 16 + k, carry)
        return carry

    def link_par(first, wide):
        def some(i, carry):
            for j in range(16 // wide):
                source = i * (16 // wide) + j
                for k in range(wide):
                    r = key((1 - yh) * 8 + source, first + k, 1000)
                    carry = link(r, 128 + first * 8 + source * wide + k, carry)
            return carry

        return some

    carry = jnp.where(rows >= 2000, 0, rows), position
    carry = lax.fori_loop(0, 8, link_own, carry)
    for first, wide in LEVELS:
        carry = lax.fori_loop(0, wide // 2, link_par(first, wide), carry)
    before, last = carry
    order_v[:8] = before
    order_v[8:] = last
    order_to_smem = pltpu.make_async_copy(order_v, order_s, loc.at[15])
    order_to_smem.start()

    for part in range(4):
        get_t(part).wait()

        def halves(t, carry, part=part):
            hi, lo = split(raw_t[part % 2, t])
            t_v[part * 64 + t, :, :TILE] = hi
            t_v[part * 64 + t, :, TILE:] = lo
            return carry

        lax.fori_loop(0, 64, halves, 0)
        if part < 2:
            get_t(part + 2).start()
    order_to_smem.wait()

    def send2(f, n, to):
        return pltpu.make_async_remote_copy(
            src_ref=ysend.at[f, to],
            dst_ref=y4[f].at[pl.ds(pl.multiple_of(n * 8, 8), 8)],
            send_sem=s2.at[f, to], recv_sem=r2.at[f, n],
            device_id=(blk, to), device_id_type=MESH,
        )

    def own2(f):
        return pltpu.make_async_copy(
            ysend.at[f, nar], y4[f].at[pl.ds(pl.multiple_of(nar * 8, 8), 8)], loc.at[6 + f]
        )

    w_rows = w_v[...].T
    w_parts = []
    for f in range(F):
        hi, lo = split(
            jnp.concatenate([w_rows[n * 32 + f * 8 : n * 32 + f * 8 + 8] for n in range(8)], axis=0)
        )
        w_parts.append((jnp.concatenate([hi, lo], axis=0), hi))

    get_own.wait()
    for step, other in NARROW:
        n = narrow_peer(step, other)
        send1(n, n).wait_recv()
    halves_x = [split(xt[:, half * 512 : half * 512 + 512]) for half in range(2)]
    for f in range(F):
        both, hi = w_parts[f]
        for half, (xh, xl) in enumerate(halves_x):
            y = nn_dot(both, xh)
            y = y[:64] + y[64:] + nn_dot(hi, xl)
            for b in range(4):
                scale = inv[half * 4 + b : half * 4 + b + 1, :]
                for n in range(8):
                    ysend[f, n, half * 4 + b] = (
                        y[n * 8 : n * 8 + 8, b * TILE : (b + 1) * TILE] * scale
                    )
        for step, other in NARROW:
            send2(f, nar, narrow_peer(step, other)).start()
        own2(f).start()

    get_list.wait()
    for step, other in ROW:
        send_list(step, other).wait_recv()
    for g in (2, 3):
        list_across(g).wait_recv()
    to_smem = pltpu.make_async_copy(lists_v, lists_s, loc.at[10])
    to_smem.start()
    to_smem.wait()

    def send_y(f):
        return pltpu.make_async_remote_copy(
            src_ref=y4[f], dst_ref=yp[f], send_sem=sy.at[f], recv_sem=ry.at[f],
            device_id=(partner, nar), device_id_type=MESH,
        )

    def send_blocks(buf, got, ssem, rsem, part, source, step, other):
        slot = step * 2 + other
        return pltpu.make_async_remote_copy(
            src_ref=buf.at[part, slot], dst_ref=got.at[part, source],
            send_sem=ssem.at[part, slot], recv_sem=rsem.at[part, source],
            device_id=(yh * 8 + row_peer(step, other), nar), device_id_type=MESH,
        )

    def column(slot, source, k):
        return lists_s[slot, source, k]

    def send_own(f, source, step, other):
        return send_blocks(own_b, got_own, so, ro, f, source, step, other)

    def send_early(f, source, step, other):
        return send_blocks(early_b, got_early, se, re, f, source, step, other)

    def send_late(level, source, step, other):
        first, wide = LEVELS[level]
        slot = step * 2 + other
        pairs = pl.ds(first // 2, wide // 2)
        return pltpu.make_async_remote_copy(
            src_ref=late_b.at[pairs, slot], dst_ref=got_late.at[pairs, source],
            send_sem=sq.at[level, slot], recv_sem=rq.at[level, source],
            device_id=(yh * 8 + row_peer(step, other), nar), device_id_type=MESH,
        )

    lane = lax.broadcasted_iota(jnp.int32, (8, TILE), 1)

    def swap_hub(source):
        return pltpu.make_async_remote_copy(
            src_ref=hub_v, dst_ref=hub_in.at[source], send_sem=sh.at[16], recv_sem=rh.at[source],
            device_id=(partner, nar), device_id_type=MESH,
        )

    def send_hub(src, source, sem, step, other):
        return pltpu.make_async_remote_copy(
            src_ref=src, dst_ref=hub_in.at[source], send_sem=sh.at[sem],
            recv_sem=rh.at[source],
            device_id=(yh * 8 + row_peer(step, other), nar), device_id_type=MESH,
        )

    rows_of = (ya, row1, row2, row3)

    def spread(step):
        return pltpu.make_async_remote_copy(
            src_ref=ya, dst_ref=rows_of[step], send_sem=sb.at[step], recv_sem=rb.at[step],
            device_id=(yh * 8 + row_peer(4 - step, 0), nar), device_id_type=MESH,
        )

    def relay(step):
        half = pl.ds(0 if step == 1 else 32, 32)
        return pltpu.make_async_remote_copy(
            src_ref=rows_of[step].at[half], dst_ref=row2.at[half],
            send_sem=sb.at[step - 1], recv_sem=rb.at[step - 1],
            device_id=(yh * 8 + row_peer(4 - step, 0), nar), device_id_type=MESH,
        )

    def send_first(g):
        return pltpu.make_async_remote_copy(
            src_ref=sel_b.at[g], dst_ref=got_first.at[g], send_sem=sf.at[g], recv_sem=rf.at[g],
            device_id=(chip[g], nar), device_id_type=MESH,
        )

    for f in range(F):
        own2(f).wait()
        for step, other in NARROW:
            n = narrow_peer(step, other)
            send2(f, n, n).wait_recv()
        if f == F - 1:
            hub = jnp.zeros((8, TILE), jnp.float32)
            for h in range(8):
                node = hubs[0, h]
                here = lane == lax.rem(node, TILE)
                for g in range(F):
                    col = jnp.sum(jnp.where(here, y4[g][node // TILE], 0.0), axis=1, keepdims=True)
                    hub = jnp.where(lane == g * 8 + h, col, hub)
            hub_v[...] = hub
            hub_in[blk] = hub
            swap_hub(blk).start()
            for step, other in ROW:
                send_hub(hub_v, blk, step * 2 + other, step, other).start()
        if f == 0:
            for step in (1, 3):
                spread(step).start()
            continue
        send_y(f).start()
        for step, other in ROW:
            slot = step * 2 + other
            for k in range(SLOTS):
                own_b[f - 1, slot, k] = y4[f][column(slot, blk, k)]
            send_own(f - 1, me, step, other).start()
        for k in range(SLOTS):
            got_own[f - 1, me, k] = y4[f][column(0, blk, k)]
        if f == 1:
            for step in (1, 3):
                spread(step).wait_recv()
                relay(step).start()

    for step in (1, 3):
        relay(step).wait_recv()
    for g, slot in ((2, 8), (3, 9), (1, 1), (0, 0)):
        for step in range(4):
            source = yh * 8 + row_peer(step, 0)
            for k in range(SLOTS):
                picked = rows_of[step][column(slot, source, k)]
                if g == 0:
                    got_first[g, step, k] = picked
                else:
                    sel_b[g, step, k] = picked
        if g > 0:
            send_first(g).start()

    def first_at(g, i, k):
        return got_first[g + lax.rem(i % 2 + core, 2), lax.rem(i // 2 - x + 4, 4), k]

    def keep_y(b, carry):
        for f in range(F):
            value[b, f] = y4[f][b]
        return carry

    lax.fori_loop(0, BLOCKS, keep_y, 0)
    swap_hub(partner).wait_recv()
    for step, other in ROW:
        send_hub(hub_in.at[partner], partner, 8 + step * 2 + other, step, other).start()

    send_y(1).wait_recv()
    for step, other in ROW:
        slot = step * 2 + other
        for k in range(SLOTS):
            early_b[0, slot, k] = yp[1][column(slot, partner, k)]
        send_early(0, me, step, other).start()
    for k in range(SLOTS):
        got_early[0, me, k] = yp[1][column(0, partner, k)]


    def product(xs, t):
        xh, xl = split(xs)
        x2 = jnp.concatenate(
            [
                jnp.concatenate([xh, xh], axis=1),
                jnp.concatenate([xl, jnp.zeros_like(xl)], axis=1),
            ],
            axis=0,
        )
        p = nt_dot(x2, t_v[t])
        return p[:32] + p[32:]

    def add(products, first):
        for j, p in enumerate(products):
            s = first + j
            back = order_s[s // TILE, lax.rem(s, TILE)]
            for f in range(F):
                value[BLOCKS + s, f] = p[f * 8 : f * 8 + 8, :] + value[back, f]

    def own_products(i, carry):
        for half in range(2):
            products = []
            for k in range(half * 8, half * 8 + 8):
                xs = jnp.concatenate([first_at(0, i, k)] + [got_own[f, i, k] for f in range(F - 1)], axis=0)
                products.append(product(xs, my_list[0, 2, yh * 8 + i, k]))
            add(products, i * 16 + half * 8)
        return carry

    def par_products(first, wide):
        def some(i, carry):
            products = []
            for j in range(8 // wide):
                source = i * (8 // wide) + j
                for k in range(first, first + wide):
                    xs = jnp.concatenate(
                        [first_at(2, source, k), got_early[0, source, k]]
                        + [got_late[k // 2, source, f, k % 2] for f in range(2)],
                        axis=0,
                    )
                    products.append(product(xs, my_list[0, 2, (1 - yh) * 8 + source, k]))
            add(products, 128 + first * 8 + i * 8)
            return carry

        lax.fori_loop(0, wide, some, 0)

    for f in range(2, F):
        send_y(f).wait_recv()

    def start_late(level):
        first, wide = LEVELS[level]
        for step, other in ROW:
            slot = step * 2 + other
            for k in range(first, first + wide):
                c = column(slot, partner, k)
                for f in range(2):
                    late_b[k // 2, slot, f, k % 2] = yp[2 + f][c]
            send_late(level, me, step, other).start()
        for k in range(first, first + wide):
            c = column(0, partner, k)
            for f in range(2):
                got_late[k // 2, me, f, k % 2] = yp[2 + f][c]

    def late_done(level):
        for step, other in ROW:
            send_late(level, row_peer(step, other), step, other).wait()

    for level in range(len(LEVELS)):
        start_late(level)
    for f in range(F - 1):
        for step, other in ROW:
            send_own(f, row_peer(step, other), step, other).wait()
    send_first(1).wait_recv()
    lax.fori_loop(0, 8, own_products, 0)

    for step, other in ROW:
        peer = row_peer(step, other)
        for o in (yh * 8 + peer, (1 - yh) * 8 + peer):
            send_hub(hub_v, o, 0, step, other).wait_recv()
    parts = []
    for f in range(F):
        total = jnp.zeros((8, TILE), jnp.float32)
        for o in range(16):
            moved = pltpu.roll(hub_in[o], (o * 8 - f * 8) % TILE, 1)
            total = jnp.where(lane // 8 == o, moved, total)
        parts.append(total)
    gh, gl = split(jnp.concatenate(parts, axis=0))
    g2 = jnp.concatenate([gh, gl], axis=0)
    get_hw.wait()

    def hub_sum(i, carry):
        hh, hl = split(hw_v[:, pl.ds(pl.multiple_of(i * 512, 512), 512)])
        p = nn_dot(g2, hh)
        p = p[:32] + p[32:] + nn_dot(gh, hl)
        for b in range(4):
            for f in range(F):
                hub_sums[i * 4 + b, f] = p[f * 8 : f * 8 + 8, b * TILE : (b + 1) * TILE]
        return carry

    lax.fori_loop(0, 16, hub_sum, 0)

    for f in range(F):
        if f > 0:
            send_y(f).wait_send()
        for step, other in NARROW:
            n = narrow_peer(step, other)
            send2(f, n, n).wait_send()
    for step, other in NARROW:
        n = narrow_peer(step, other)
        send1(n, n).wait_send()
    for step, other in ROW:
        send_list(step, other).wait_send()
    for g in (2, 3):
        list_across(g).wait_send()
    swap_hub(partner).wait_send()
    for step, other in ROW:
        send_hub(hub_v, blk, step * 2 + other, step, other).wait_send()
        send_hub(hub_v, blk, 8 + step * 2 + other, step, other).wait_send()
    for step, other in ROW:
        send_early(0, row_peer(step, other), step, other).wait()
    for step in (1, 3):
        spread(step).wait_send()
        relay(step).wait_send()
    for g in (1, 2, 3):
        send_first(g).wait_send()
    for g in (2, 3):
        send_first(g).wait_recv()
    for level in range(len(LEVELS)):
        late_done(level)
        par_products(*LEVELS[level])

    sub = lax.broadcasted_iota(jnp.int32, (8, TILE), 0)
    biases = []
    for f in range(F):
        column_f = jnp.zeros((8, TILE), jnp.float32)
        for i in range(8):
            column_f = jnp.where(sub == i, bias[nar * 32 + f * 8 + i], column_f)
        biases.append(column_f)

    def finish(i, carry):
        inv = lax.rsqrt(deg_v[pl.ds(pl.multiple_of(i * 8, 8), 8), :].astype(jnp.float32))
        for b in range(8):
            end = order_s[8, i * 8 + b]
            for f in range(F):
                out[f * 8 : f * 8 + 8, pl.ds(pl.multiple_of((i * 8 + b) * TILE, TILE), TILE)] = (
                    jnp.maximum(
                        (value[end, f] + hub_sums[i * 8 + b, f]) * inv[b : b + 1, :] + biases[f],
                        0.0,
                    )
                )
        return carry

    def put(i):
        here = pl.ds(i * 2048, 2048)
        return pltpu.make_async_copy(out.at[:, here], out_hbm.at[:, here], loc.at[i])

    for i in range(4):
        lax.fori_loop(i * 2, i * 2 + 2, finish, 0)
        put(i).start()
    for i in range(4):
        put(i).wait()


def exchange(feat, deg, weight, lists, counts, hubs, bias, tiles, hub_w):
    f32, bf16 = jnp.float32, jnp.bfloat16
    dma = pltpu.SemaphoreType.DMA
    vmem = pltpu.VMEM
    smem = pl.BlockSpec(memory_space=pltpu.SMEM)
    hbm = pl.BlockSpec(memory_space=pl.ANY)
    tile = (8, TILE)
    return pl.pallas_call(
        exchange_kernel,
        out_shape=jax.ShapeDtypeStruct((32, BLOCKS * TILE), f32),
        in_specs=[hbm, hbm, hbm, hbm, smem, smem, smem, smem, hbm, hbm],
        out_specs=hbm,
        scratch_shapes=[
            vmem((256, 1024), f32),
            vmem((F, 8, 8, *tile), f32),
            *[vmem((BLOCKS, *tile), f32)] * 7,
            vmem((F - 1, 8, SLOTS, *tile), f32),
            vmem((1, 8, SLOTS, *tile), f32),
            vmem((8, 8, 2, 2, *tile), f32),
            *[vmem((BLOCKS, *tile), f32)] * 3,
            vmem((4, 4, SLOTS, *tile), f32),
            vmem((4, 4, SLOTS, *tile), f32),
            vmem((F - 1, 8, SLOTS, *tile), f32),
            vmem((1, 8, SLOTS, *tile), f32),
            vmem((8, 8, 2, 2, *tile), f32),
            vmem((10, 16, SLOTS), jnp.int32),
            pltpu.SMEM((10, 16, SLOTS), jnp.int32),
            vmem(tile, f32),
            vmem((16, *tile), f32),
            vmem((BLOCKS, TILE), jnp.int32),
            vmem((256, 256), f32),
            vmem((2, 64, TILE, TILE), f32),
            vmem((TV, TILE, 2 * TILE), bf16),
            vmem((128, BLOCKS * TILE), f32),
            vmem((16, TILE), jnp.int32),
            pltpu.SMEM((16, TILE), jnp.int32),
            vmem((BLOCKS + TV, F, *tile), f32),
            vmem((BLOCKS, F, *tile), f32),
            vmem((32, BLOCKS * TILE), f32),
            dma((8,)), dma((8,)),
            dma((F, 8)), dma((F, 8)),
            dma((F,)), dma((F,)),
            dma((10,)), dma((10,)),
            dma((17,)), dma((16,)),
            dma((F - 1, 8)), dma((F - 1, 8)),
            dma((1, 8)), dma((1, 8)),
            dma((len(LEVELS), 8)), dma((len(LEVELS), 8)),
            dma((4,)), dma((4,)),
            dma((4,)), dma((4,)),
            dma((16,)),
        ],
        compiler_params=pltpu.CompilerParams(
            collective_id=0, has_side_effects=True, vmem_limit_bytes=60 * 2**20
        ),
    )(feat, deg, weight, lists, lists, counts, hubs, bias, tiles, hub_w)


def body(
    features, degrees, tile_values, tile_list, tile_count, hub_local, hub_weights, weight, out_bias
):
    deg = degrees.reshape(BLOCKS, TILE)
    lists = jnp.transpose(tile_list, (0, 2, 1, 3))
    return exchange(
        features, deg, weight, lists, tile_count, hub_local, out_bias, tile_values, hub_weights
    )


def solution(mesh):
    return jax.shard_map(
        body,
        mesh=mesh,
        in_specs=(
            P("narrow", "blk"),
            P("blk"),
            P("blk", None, None),
            P("blk", None, None, None),
            P("blk", None),
            P("blk", None),
            P(None, "blk"),
            P(),
            P(),
        ),
        out_specs=P("narrow", "blk"),
        check_vma=False,
    )
```

```python
import functools

import jax
import jax.numpy as jnp
from jax import lax
from jax.experimental import pallas as pl
from jax.experimental.pallas import tpu as pltpu
from jax.sharding import PartitionSpec as P

TILE = 128
SLOTS = 16
F = 4
BLOCKS = 64
TV = 256
LEVELS = ((0, 4), (4, 4), (8, 4), (12, 2), (14, 2))
MESH = pl.DeviceIdType.MESH
ROW = ((2, 0), (2, 1), (1, 0), (3, 0), (1, 1), (3, 1), (0, 1))
FAR = ((2, 1), (1, 1), (3, 1), (0, 1), (2, 0), (1, 0), (3, 0))
NARROW = ((1, 0), (3, 0), (0, 1), (2, 0), (1, 1), (3, 1), (2, 1))


def split(x):
    hi = x.astype(jnp.bfloat16)
    lo = (x - hi.astype(jnp.float32)).astype(jnp.bfloat16)
    return hi, lo


def nt_dot(a, b):
    return lax.dot_general(a, b, (((1,), (1,)), ((), ())), preferred_element_type=jnp.float32)


def nn_dot(a, b):
    return jnp.dot(a, b, preferred_element_type=jnp.float32)


def exchange_kernel(
    feat, deg, weight, lists, my_list, counts, hubs, bias, tiles, hub_w,
    out_hbm,
    xt, ysend, ya, yb, yc, yd, pb, pc, pd, own_b, early_b, late_b,
    row1, row2, row3, sel_b, got_first,
    got_own, got_early, got_late, lists_v, lists_s, hub_v, hub_in, deg_v, w_v, raw_t, t_v, hw_v,
    order_v, order_s, value, hub_sums, out,
    s1, r1, s2, r2, sy, ry, sl, rl, sh, rh, so, ro, se, re, sq, rq, sb, rb, sf, rf, loc,
):
    y4, yp = (ya, yb, yc, yd), (None, pb, pc, pd)
    blk = lax.axis_index("blk")
    nar = lax.axis_index("narrow")
    yh, x, core = blk // 8, (blk // 2) % 4, blk % 2
    z, yl = nar // 2, nar % 2
    me = x * 2 + core
    partner = (1 - yh) * 8 + me

    def row_peer(step, other):
        return lax.rem(x + step, 4) * 2 + lax.rem(core + other, 2)

    def narrow_peer(step, other):
        return lax.rem(z + step, 4) * 2 + lax.rem(yl + other, 2)

    bar = pltpu.get_barrier_semaphore()
    for step, other in NARROW:
        pl.semaphore_signal(
            bar, inc=1, device_id=(blk, narrow_peer(step, other)), device_id_type=MESH
        )
    for step, other in ROW:
        pl.semaphore_signal(
            bar, inc=1, device_id=(yh * 8 + row_peer(step, other), nar), device_id_type=MESH
        )
    chip = (None, blk - core + 1 - core, partner, partner - core + 1 - core)
    for to in chip[2:]:
        pl.semaphore_signal(bar, inc=1, device_id=(to, nar), device_id_type=MESH)

    get_deg = pltpu.make_async_copy(deg, deg_v, loc.at[0])
    get_w = pltpu.make_async_copy(weight, w_v, loc.at[1])
    get_own = pltpu.make_async_copy(
        feat.at[:, pl.ds(pl.multiple_of(nar * 1024, 1024), 1024)],
        xt.at[pl.ds(pl.multiple_of(nar * 32, 32), 32), :], loc.at[2],
    )
    get_list = pltpu.make_async_copy(lists.at[0, 1], lists_v.at[0], loc.at[3])
    def get_t(part):
        return pltpu.make_async_copy(
            tiles.at[pl.ds(part * 64, 64)], raw_t.at[part % 2], loc.at[11 + part]
        )

    get_hw = pltpu.make_async_copy(hub_w, hw_v, loc.at[5])
    for copy in (get_w, get_deg, get_own, get_list):
        copy.start()
    pl.semaphore_wait(bar, 16)

    def send1(n, to):
        return pltpu.make_async_remote_copy(
            src_ref=feat.at[:, pl.ds(pl.multiple_of(to * 1024, 1024), 1024)],
            dst_ref=xt.at[pl.ds(pl.multiple_of(n * 32, 32), 32), :],
            send_sem=s1.at[to], recv_sem=r1.at[n],
            device_id=(blk, to), device_id_type=MESH,
        )

    for step, other in FAR:
        send1(nar, narrow_peer(step, other)).start()

    def send_list(step, other):
        slot = step * 2 + other
        return pltpu.make_async_remote_copy(
            src_ref=lists.at[0, 1], dst_ref=lists_v.at[slot],
            send_sem=sl.at[slot], recv_sem=rl.at[slot],
            device_id=(yh * 8 + row_peer(4 - step, other), nar), device_id_type=MESH,
        )

    def list_across(g):
        return pltpu.make_async_remote_copy(
            src_ref=lists.at[0, 1], dst_ref=lists_v.at[6 + g],
            send_sem=sl.at[6 + g], recv_sem=rl.at[6 + g],
            device_id=(chip[g], nar), device_id_type=MESH,
        )

    for step, other in ROW:
        send_list(step, other).start()
    for g in (2, 3):
        list_across(g).start()
    get_t(0).start()
    get_t(1).start()
    get_hw.start()

    get_w.wait()
    get_deg.wait()
    inv = lax.rsqrt(deg_v[pl.ds(pl.multiple_of(nar * 8, 8), 8), :].astype(jnp.float32))

    position = lax.broadcasted_iota(jnp.int32, (8, TILE), 0) * TILE + lax.broadcasted_iota(
        jnp.int32, (8, TILE), 1
    )

    def key(o, k, dead):
        r = my_list[0, 0, o, k]
        return jnp.where(k < counts[0, o], r, dead + r)

    def fill_own(i, rows):
        for k in range(SLOTS):
            rows = jnp.where(position == i * 16 + k, key(yh * 8 + i, k, 2000), rows)
        return rows

    def fill_par(i, rows):
        for first, wide in LEVELS:
            for k in range(wide):
                s = 128 + first * 8 + i * wide + k
                rows = jnp.where(position == s, key((1 - yh) * 8 + i, first + k, 2000), rows)
        return rows

    rows = lax.fori_loop(0, 8, fill_own, jnp.zeros((8, TILE), jnp.int32))
    rows = lax.fori_loop(0, 8, fill_par, rows)

    def link(r, s, carry):
        before, last = carry
        before = jnp.where((rows == r) & (position > s), BLOCKS + s, before)
        return before, jnp.where(position == r, BLOCKS + s, last)

    def link_own(i, carry):
        for k in range(SLOTS):
            carry = link(key(yh * 8 + i, k, 1000), i * 16 + k, carry)
        return carry

    def link_par(first, wide):
        def some(i, carry):
            for j in range(16 // wide):
                source = i * (16 // wide) + j
                for k in range(wide):
                    r = key((1 - yh) * 8 + source, first + k, 1000)
                    carry = link(r, 128 + first * 8 + source * wide + k, carry)
            return carry

        return some

    carry = jnp.where(rows >= 2000, 0, rows), position
    carry = lax.fori_loop(0, 8, link_own, carry)
    for first, wide in LEVELS:
        carry = lax.fori_loop(0, wide // 2, link_par(first, wide), carry)
    before, last = carry
    order_v[:8] = before
    order_v[8:] = last
    order_to_smem = pltpu.make_async_copy(order_v, order_s, loc.at[15])
    order_to_smem.start()

    for part in range(4):
        get_t(part).wait()

        def halves(t, carry, part=part):
            hi, lo = split(raw_t[part % 2, t])
            t_v[part * 64 + t, :, :TILE] = hi
            t_v[part * 64 + t, :, TILE:] = lo
            return carry

        lax.fori_loop(0, 64, halves, 0)
        if part < 2:
            get_t(part + 2).start()
    order_to_smem.wait()

    def send2(f, n, to):
        return pltpu.make_async_remote_copy(
            src_ref=ysend.at[f, to],
            dst_ref=y4[f].at[pl.ds(pl.multiple_of(n * 8, 8), 8)],
            send_sem=s2.at[f, to], recv_sem=r2.at[f, n],
            device_id=(blk, to), device_id_type=MESH,
        )

    def own2(f):
        return pltpu.make_async_copy(
            ysend.at[f, nar], y4[f].at[pl.ds(pl.multiple_of(nar * 8, 8), 8)], loc.at[6 + f]
        )

    w_rows = w_v[...].T
    w_parts = []
    for f in range(F):
        hi, lo = split(
            jnp.concatenate([w_rows[n * 32 + f * 8 : n * 32 + f * 8 + 8] for n in range(8)], axis=0)
        )
        w_parts.append((jnp.concatenate([hi, lo], axis=0), hi))

    get_own.wait()
    for step, other in NARROW:
        n = narrow_peer(step, other)
        send1(n, n).wait_recv()
    halves_x = [split(xt[:, half * 512 : half * 512 + 512]) for half in range(2)]
    for f in range(F):
        both, hi = w_parts[f]
        for half, (xh, xl) in enumerate(halves_x):
            y = nn_dot(both, xh)
            y = y[:64] + y[64:] + nn_dot(hi, xl)
            for b in range(4):
                scale = inv[half * 4 + b : half * 4 + b + 1, :]
                for n in range(8):
                    ysend[f, n, half * 4 + b] = (
                        y[n * 8 : n * 8 + 8, b * TILE : (b + 1) * TILE] * scale
                    )
        for step, other in NARROW:
            send2(f, nar, narrow_peer(step, other)).start()
        own2(f).start()

    get_list.wait()
    for step, other in ROW:
        send_list(step, other).wait_recv()
    for g in (2, 3):
        list_across(g).wait_recv()
    to_smem = pltpu.make_async_copy(lists_v, lists_s, loc.at[10])
    to_smem.start()
    to_smem.wait()

    def send_y(f):
        return pltpu.make_async_remote_copy(
            src_ref=y4[f], dst_ref=yp[f], send_sem=sy.at[f], recv_sem=ry.at[f],
            device_id=(partner, nar), device_id_type=MESH,
        )

    def send_blocks(buf, got, ssem, rsem, part, source, step, other):
        slot = step * 2 + other
        return pltpu.make_async_remote_copy(
            src_ref=buf.at[part, slot], dst_ref=got.at[part, source],
            send_sem=ssem.at[part, slot], recv_sem=rsem.at[part, source],
            device_id=(yh * 8 + row_peer(step, other), nar), device_id_type=MESH,
        )

    def column(slot, source, k):
        return lists_s[slot, source, k]

    def send_own(f, source, step, other):
        return send_blocks(own_b, got_own, so, ro, f, source, step, other)

    def send_early(f, source, step, other):
        return send_blocks(early_b, got_early, se, re, f, source, step, other)

    def send_late(level, source, step, other):
        first, wide = LEVELS[level]
        slot = step * 2 + other
        pairs = pl.ds(first // 2, wide // 2)
        return pltpu.make_async_remote_copy(
            src_ref=late_b.at[pairs, slot], dst_ref=got_late.at[pairs, source],
            send_sem=sq.at[level, slot], recv_sem=rq.at[level, source],
            device_id=(yh * 8 + row_peer(step, other), nar), device_id_type=MESH,
        )

    lane = lax.broadcasted_iota(jnp.int32, (8, TILE), 1)

    def swap_hub(source):
        return pltpu.make_async_remote_copy(
            src_ref=hub_v, dst_ref=hub_in.at[source], send_sem=sh.at[16], recv_sem=rh.at[source],
            device_id=(partner, nar), device_id_type=MESH,
        )

    def send_hub(src, source, sem, step, other):
        return pltpu.make_async_remote_copy(
            src_ref=src, dst_ref=hub_in.at[source], send_sem=sh.at[sem],
            recv_sem=rh.at[source],
            device_id=(yh * 8 + row_peer(step, other), nar), device_id_type=MESH,
        )

    rows_of = (ya, row1, row2, row3)

    def spread(step):
        return pltpu.make_async_remote_copy(
            src_ref=ya, dst_ref=rows_of[step], send_sem=sb.at[step], recv_sem=rb.at[step],
            device_id=(yh * 8 + row_peer(4 - step, 0), nar), device_id_type=MESH,
        )

    def relay(step):
        half = pl.ds(0 if step == 1 else 32, 32)
        return pltpu.make_async_remote_copy(
            src_ref=rows_of[step].at[half], dst_ref=row2.at[half],
            send_sem=sb.at[step - 1], recv_sem=rb.at[step - 1],
            device_id=(yh * 8 + row_peer(4 - step, 0), nar), device_id_type=MESH,
        )

    def send_first(g):
        return pltpu.make_async_remote_copy(
            src_ref=sel_b.at[g], dst_ref=got_first.at[g], send_sem=sf.at[g], recv_sem=rf.at[g],
            device_id=(chip[g], nar), device_id_type=MESH,
        )

    for f in range(F):
        own2(f).wait()
        for step, other in NARROW:
            n = narrow_peer(step, other)
            send2(f, n, n).wait_recv()
        if f == F - 1:
            hub = jnp.zeros((8, TILE), jnp.float32)
            for h in range(8):
                node = hubs[0, h]
                here = lane == lax.rem(node, TILE)
                for g in range(F):
                    col = jnp.sum(jnp.where(here, y4[g][node // TILE], 0.0), axis=1, keepdims=True)
                    hub = jnp.where(lane == g * 8 + h, col, hub)
            hub_v[...] = hub
            hub_in[blk] = hub
            swap_hub(blk).start()
            for step, other in ROW:
                send_hub(hub_v, blk, step * 2 + other, step, other).start()
        if f == 0:
            for step in (1, 3):
                spread(step).start()
            continue
        send_y(f).start()
        for step, other in ROW:
            slot = step * 2 + other
            for k in range(SLOTS):
                own_b[f - 1, slot, k] = y4[f][column(slot, blk, k)]
            send_own(f - 1, me, step, other).start()
        for k in range(SLOTS):
            got_own[f - 1, me, k] = y4[f][column(0, blk, k)]
        if f == 1:
            for step in (1, 3):
                spread(step).wait_recv()
                relay(step).start()

    for step in (1, 3):
        relay(step).wait_recv()
    for g, slot in ((2, 8), (3, 9), (1, 1), (0, 0)):
        for step in range(4):
            source = yh * 8 + row_peer(step, 0)
            for k in range(SLOTS):
                picked = rows_of[step][column(slot, source, k)]
                if g == 0:
                    got_first[g, step, k] = picked
                else:
                    sel_b[g, step, k] = picked
        if g > 0:
            send_first(g).start()

    def first_at(g, i, k):
        return got_first[g + lax.rem(i % 2 + core, 2), lax.rem(i // 2 - x + 4, 4), k]

    def keep_y(b, carry):
        for f in range(F):
            value[b, f] = y4[f][b]
        return carry

    lax.fori_loop(0, BLOCKS, keep_y, 0)
    swap_hub(partner).wait_recv()
    for step, other in ROW:
        send_hub(hub_in.at[partner], partner, 8 + step * 2 + other, step, other).start()

    send_y(1).wait_recv()
    for step, other in ROW:
        slot = step * 2 + other
        for k in range(SLOTS):
            early_b[0, slot, k] = yp[1][column(slot, partner, k)]
        send_early(0, me, step, other).start()
    for k in range(SLOTS):
        got_early[0, me, k] = yp[1][column(0, partner, k)]


    def product(xs, t):
        xh, xl = split(xs)
        x2 = jnp.concatenate(
            [
                jnp.concatenate([xh, xh], axis=1),
                jnp.concatenate([xl, jnp.zeros_like(xl)], axis=1),
            ],
            axis=0,
        )
        p = nt_dot(x2, t_v[t])
        return p[:32] + p[32:]

    def add(products, first):
        for j, p in enumerate(products):
            s = first + j
            back = order_s[s // TILE, lax.rem(s, TILE)]
            for f in range(F):
                value[BLOCKS + s, f] = p[f * 8 : f * 8 + 8, :] + value[back, f]

    def own_products(i, carry):
        for half in range(2):
            products = []
            for k in range(half * 8, half * 8 + 8):
                xs = jnp.concatenate([first_at(0, i, k)] + [got_own[f, i, k] for f in range(F - 1)], axis=0)
                products.append(product(xs, my_list[0, 2, yh * 8 + i, k]))
            add(products, i * 16 + half * 8)
        return carry

    def par_products(first, wide):
        def some(i, carry):
            products = []
            for j in range(8 // wide):
                source = i * (8 // wide) + j
                for k in range(first, first + wide):
                    xs = jnp.concatenate(
                        [first_at(2, source, k), got_early[0, source, k]]
                        + [got_late[k // 2, source, f, k % 2] for f in range(2)],
                        axis=0,
                    )
                    products.append(product(xs, my_list[0, 2, (1 - yh) * 8 + source, k]))
            add(products, 128 + first * 8 + i * 8)
            return carry

        lax.fori_loop(0, wide, some, 0)

    for f in range(2, F):
        send_y(f).wait_recv()

    def start_late(level):
        first, wide = LEVELS[level]
        for step, other in ROW:
            slot = step * 2 + other
            for k in range(first, first + wide):
                c = column(slot, partner, k)
                for f in range(2):
                    late_b[k // 2, slot, f, k % 2] = yp[2 + f][c]
            send_late(level, me, step, other).start()
        for k in range(first, first + wide):
            c = column(0, partner, k)
            for f in range(2):
                got_late[k // 2, me, f, k % 2] = yp[2 + f][c]

    def late_done(level):
        for step, other in ROW:
            send_late(level, row_peer(step, other), step, other).wait()

    for level in range(len(LEVELS)):
        start_late(level)
    for f in range(F - 1):
        for step, other in ROW:
            send_own(f, row_peer(step, other), step, other).wait()
    send_first(1).wait_recv()
    lax.fori_loop(0, 8, own_products, 0)

    for step, other in ROW:
        peer = row_peer(step, other)
        for o in (yh * 8 + peer, (1 - yh) * 8 + peer):
            send_hub(hub_v, o, 0, step, other).wait_recv()
    parts = []
    for f in range(F):
        total = jnp.zeros((8, TILE), jnp.float32)
        for o in range(16):
            moved = pltpu.roll(hub_in[o], (o * 8 - f * 8) % TILE, 1)
            total = jnp.where(lane // 8 == o, moved, total)
        parts.append(total)
    gh, gl = split(jnp.concatenate(parts, axis=0))
    g2 = jnp.concatenate([gh, gl], axis=0)
    get_hw.wait()

    def hub_sum(i, carry):
        hh, hl = split(hw_v[:, pl.ds(pl.multiple_of(i * 512, 512), 512)])
        p = nn_dot(g2, hh)
        p = p[:32] + p[32:] + nn_dot(gh, hl)
        for b in range(4):
            for f in range(F):
                hub_sums[i * 4 + b, f] = p[f * 8 : f * 8 + 8, b * TILE : (b + 1) * TILE]
        return carry

    lax.fori_loop(0, 16, hub_sum, 0)

    for f in range(F):
        if f > 0:
            send_y(f).wait_send()
        for step, other in NARROW:
            n = narrow_peer(step, other)
            send2(f, n, n).wait_send()
    for step, other in NARROW:
        n = narrow_peer(step, other)
        send1(n, n).wait_send()
    for step, other in ROW:
        send_list(step, other).wait_send()
    for g in (2, 3):
        list_across(g).wait_send()
    swap_hub(partner).wait_send()
    for step, other in ROW:
        send_hub(hub_v, blk, step * 2 + other, step, other).wait_send()
        send_hub(hub_v, blk, 8 + step * 2 + other, step, other).wait_send()
    for step, other in ROW:
        send_early(0, row_peer(step, other), step, other).wait()
    for step in (1, 3):
        spread(step).wait_send()
        relay(step).wait_send()
    for g in (1, 2, 3):
        send_first(g).wait_send()
    for g in (2, 3):
        send_first(g).wait_recv()
    for level in range(len(LEVELS)):
        late_done(level)
        par_products(*LEVELS[level])

    sub = lax.broadcasted_iota(jnp.int32, (8, TILE), 0)
    biases = []
    for f in range(F):
        column_f = jnp.zeros((8, TILE), jnp.float32)
        for i in range(8):
            column_f = jnp.where(sub == i, bias[nar * 32 + f * 8 + i], column_f)
        biases.append(column_f)

    def finish(i, carry):
        inv = lax.rsqrt(deg_v[pl.ds(pl.multiple_of(i * 8, 8), 8), :].astype(jnp.float32))
        for b in range(8):
            end = order_s[8, i * 8 + b]
            for f in range(F):
                out[f * 8 : f * 8 + 8, pl.ds(pl.multiple_of((i * 8 + b) * TILE, TILE), TILE)] = (
                    jnp.maximum(
                        (value[end, f] + hub_sums[i * 8 + b, f]) * inv[b : b + 1, :] + biases[f],
                        0.0,
                    )
                )
        return carry

    def put(i):
        here = pl.ds(i * 2048, 2048)
        return pltpu.make_async_copy(out.at[:, here], out_hbm.at[:, here], loc.at[i])

    for i in range(4):
        lax.fori_loop(i * 2, i * 2 + 2, finish, 0)
        put(i).start()
    for i in range(4):
        put(i).wait()


def exchange(feat, deg, weight, lists, counts, hubs, bias, tiles, hub_w):
    f32, bf16 = jnp.float32, jnp.bfloat16
    dma = pltpu.SemaphoreType.DMA
    vmem = pltpu.VMEM
    smem = pl.BlockSpec(memory_space=pltpu.SMEM)
    hbm = pl.BlockSpec(memory_space=pl.ANY)
    tile = (8, TILE)
    return pl.pallas_call(
        exchange_kernel,
        out_shape=pltpu.VMEM((32, BLOCKS * TILE), f32),
        in_specs=[hbm, hbm, hbm, hbm, smem, smem, smem, smem, hbm, hbm],
        out_specs=hbm,
        scratch_shapes=[
            vmem((256, 1024), f32),
            vmem((F, 8, 8, *tile), f32),
            *[vmem((BLOCKS, *tile), f32)] * 7,
            vmem((F - 1, 8, SLOTS, *tile), f32),
            vmem((1, 8, SLOTS, *tile), f32),
            vmem((8, 8, 2, 2, *tile), f32),
            *[vmem((BLOCKS, *tile), f32)] * 3,
            vmem((4, 4, SLOTS, *tile), f32),
            vmem((4, 4, SLOTS, *tile), f32),
            vmem((F - 1, 8, SLOTS, *tile), f32),
            vmem((1, 8, SLOTS, *tile), f32),
            vmem((8, 8, 2, 2, *tile), f32),
            vmem((10, 16, SLOTS), jnp.int32),
            pltpu.SMEM((10, 16, SLOTS), jnp.int32),
            vmem(tile, f32),
            vmem((16, *tile), f32),
            vmem((BLOCKS, TILE), jnp.int32),
            vmem((256, 256), f32),
            vmem((2, 64, TILE, TILE), f32),
            vmem((TV, TILE, 2 * TILE), bf16),
            vmem((128, BLOCKS * TILE), f32),
            vmem((16, TILE), jnp.int32),
            pltpu.SMEM((16, TILE), jnp.int32),
            vmem((BLOCKS + TV, F, *tile), f32),
            vmem((BLOCKS, F, *tile), f32),
            vmem((32, BLOCKS * TILE), f32),
            dma((8,)), dma((8,)),
            dma((F, 8)), dma((F, 8)),
            dma((F,)), dma((F,)),
            dma((10,)), dma((10,)),
            dma((17,)), dma((16,)),
            dma((F - 1, 8)), dma((F - 1, 8)),
            dma((1, 8)), dma((1, 8)),
            dma((len(LEVELS), 8)), dma((len(LEVELS), 8)),
            dma((4,)), dma((4,)),
            dma((4,)), dma((4,)),
            dma((16,)),
        ],
        compiler_params=pltpu.CompilerParams(
            collective_id=0, has_side_effects=True, vmem_limit_bytes=60 * 2**20
        ),
    )(feat, deg, weight, lists, lists, counts, hubs, bias, tiles, hub_w)


def body(
    features, degrees, tile_values, tile_list, tile_count, hub_local, hub_weights, weight, out_bias
):
    deg = degrees.reshape(BLOCKS, TILE)
    lists = jnp.transpose(tile_list, (0, 2, 1, 3))
    return exchange(
        features, deg, weight, lists, tile_count, hub_local, out_bias, tile_values, hub_weights
    )


def solution(mesh):
    return jax.shard_map(
        body,
        mesh=mesh,
        in_specs=(
            P("narrow", "blk"),
            P("blk"),
            P("blk", None, None),
            P("blk", None, None, None),
            P("blk", None),
            P("blk", None),
            P(None, "blk"),
            P(),
            P(),
        ),
        out_specs=P("narrow", "blk"),
        check_vma=False,
    )
```

```python
import functools

import jax
import jax.numpy as jnp
from jax import lax
from jax.experimental import pallas as pl
from jax.experimental.pallas import tpu as pltpu
from jax.sharding import PartitionSpec as P

TILE = 128
SLOTS = 16
F = 4
BLOCKS = 64
TV = 256
LEVELS = ((0, 4), (4, 4), (8, 4), (12, 2), (14, 2))
MESH = pl.DeviceIdType.MESH
ROW = ((1, 0), (3, 0), (1, 1), (3, 1), (2, 0), (2, 1), (0, 1))
FAR = ((2, 1), (1, 1), (3, 1), (0, 1), (2, 0), (1, 0), (3, 0))
NARROW = ((1, 0), (3, 0), (0, 1), (2, 0), (1, 1), (3, 1), (2, 1))


def split(x):
    hi = x.astype(jnp.bfloat16)
    lo = (x - hi.astype(jnp.float32)).astype(jnp.bfloat16)
    return hi, lo


def nt_dot(a, b):
    return lax.dot_general(a, b, (((1,), (1,)), ((), ())), preferred_element_type=jnp.float32)


def nn_dot(a, b):
    return jnp.dot(a, b, preferred_element_type=jnp.float32)


def exchange_kernel(
    feat, deg, weight, lists, my_list, counts, hubs, bias, tiles, hub_w,
    out,
    xt, ysend, ya, yb, yc, yd, pb, pc, pd, own_b, early_b, late_b,
    row1, row2, row3, sel_b, got_first,
    got_own, got_early, got_late, lists_v, lists_s, hub_v, hub_in, deg_v, w_v, raw_t, t_v, hw_v,
    order_v, order_s, value, hub_sums,
    s1, r1, s2, r2, sy, ry, sl, rl, sh, rh, so, ro, se, re, sq, rq, sb, rb, sf, rf, loc,
):
    y4, yp = (ya, yb, yc, yd), (None, pb, pc, pd)
    blk = lax.axis_index("blk")
    nar = lax.axis_index("narrow")
    yh, x, core = blk // 8, (blk // 2) % 4, blk % 2
    z, yl = nar // 2, nar % 2
    me = x * 2 + core
    partner = (1 - yh) * 8 + me

    def row_peer(step, other):
        return lax.rem(x + step, 4) * 2 + lax.rem(core + other, 2)

    def narrow_peer(step, other):
        return lax.rem(z + step, 4) * 2 + lax.rem(yl + other, 2)

    bar = pltpu.get_barrier_semaphore()
    for step, other in NARROW:
        pl.semaphore_signal(
            bar, inc=1, device_id=(blk, narrow_peer(step, other)), device_id_type=MESH
        )
    for step, other in ROW:
        pl.semaphore_signal(
            bar, inc=1, device_id=(yh * 8 + row_peer(step, other), nar), device_id_type=MESH
        )
    chip = (None, blk - core + 1 - core, partner, partner - core + 1 - core)
    for to in chip[2:]:
        pl.semaphore_signal(bar, inc=1, device_id=(to, nar), device_id_type=MESH)

    get_deg = pltpu.make_async_copy(deg, deg_v, loc.at[0])
    get_w = pltpu.make_async_copy(weight, w_v, loc.at[1])
    get_own = pltpu.make_async_copy(
        feat.at[:, pl.ds(pl.multiple_of(nar * 1024, 1024), 1024)],
        xt.at[pl.ds(pl.multiple_of(nar * 32, 32), 32), :], loc.at[2],
    )
    get_list = pltpu.make_async_copy(lists.at[0, 1], lists_v.at[0], loc.at[3])
    def get_t(part):
        return pltpu.make_async_copy(
            tiles.at[pl.ds(part * 64, 64)], raw_t.at[part % 2], loc.at[11 + part]
        )

    get_hw = pltpu.make_async_copy(hub_w, hw_v, loc.at[5])
    for copy in (get_w, get_deg, get_own, get_list):
        copy.start()
    pl.semaphore_wait(bar, 16)

    def send1(n, to):
        return pltpu.make_async_remote_copy(
            src_ref=feat.at[:, pl.ds(pl.multiple_of(to * 1024, 1024), 1024)],
            dst_ref=xt.at[pl.ds(pl.multiple_of(n * 32, 32), 32), :],
            send_sem=s1.at[to], recv_sem=r1.at[n],
            device_id=(blk, to), device_id_type=MESH,
        )

    for step, other in FAR:
        send1(nar, narrow_peer(step, other)).start()

    def send_list(step, other):
        slot = step * 2 + other
        return pltpu.make_async_remote_copy(
            src_ref=lists.at[0, 1], dst_ref=lists_v.at[slot],
            send_sem=sl.at[slot], recv_sem=rl.at[slot],
            device_id=(yh * 8 + row_peer(4 - step, other), nar), device_id_type=MESH,
        )

    def list_across(g):
        return pltpu.make_async_remote_copy(
            src_ref=lists.at[0, 1], dst_ref=lists_v.at[6 + g],
            send_sem=sl.at[6 + g], recv_sem=rl.at[6 + g],
            device_id=(chip[g], nar), device_id_type=MESH,
        )

    for step, other in ROW:
        send_list(step, other).start()
    for g in (2, 3):
        list_across(g).start()
    get_t(0).start()
    get_t(1).start()
    get_hw.start()

    get_w.wait()
    get_deg.wait()
    inv = lax.rsqrt(deg_v[pl.ds(pl.multiple_of(nar * 8, 8), 8), :].astype(jnp.float32))

    position = lax.broadcasted_iota(jnp.int32, (8, TILE), 0) * TILE + lax.broadcasted_iota(
        jnp.int32, (8, TILE), 1
    )

    def key(o, k, dead):
        r = my_list[0, 0, o, k]
        return jnp.where(k < counts[0, o], r, dead + r)

    def fill_own(i, rows):
        for k in range(SLOTS):
            rows = jnp.where(position == i * 16 + k, key(yh * 8 + i, k, 2000), rows)
        return rows

    def fill_par(i, rows):
        for first, wide in LEVELS:
            for k in range(wide):
                s = 128 + first * 8 + i * wide + k
                rows = jnp.where(position == s, key((1 - yh) * 8 + i, first + k, 2000), rows)
        return rows

    rows = lax.fori_loop(0, 8, fill_own, jnp.zeros((8, TILE), jnp.int32))
    rows = lax.fori_loop(0, 8, fill_par, rows)

    def link(r, s, carry):
        before, last = carry
        before = jnp.where((rows == r) & (position > s), BLOCKS + s, before)
        return before, jnp.where(position == r, BLOCKS + s, last)

    def link_own(i, carry):
        for k in range(SLOTS):
            carry = link(key(yh * 8 + i, k, 1000), i * 16 + k, carry)
        return carry

    def link_par(first, wide):
        def some(i, carry):
            for j in range(16 // wide):
                source = i * (16 // wide) + j
                for k in range(wide):
                    r = key((1 - yh) * 8 + source, first + k, 1000)
                    carry = link(r, 128 + first * 8 + source * wide + k, carry)
            return carry

        return some

    carry = jnp.where(rows >= 2000, 0, rows), position
    carry = lax.fori_loop(0, 8, link_own, carry)
    for first, wide in LEVELS:
        carry = lax.fori_loop(0, wide // 2, link_par(first, wide), carry)
    before, last = carry
    order_v[:8] = before
    order_v[8:] = last
    order_to_smem = pltpu.make_async_copy(order_v, order_s, loc.at[15])
    order_to_smem.start()

    for part in range(4):
        get_t(part).wait()

        def halves(t, carry, part=part):
            hi, lo = split(raw_t[part % 2, t])
            t_v[part * 64 + t, :, :TILE] = hi
            t_v[part * 64 + t, :, TILE:] = lo
            return carry

        lax.fori_loop(0, 64, halves, 0)
        if part < 2:
            get_t(part + 2).start()
    order_to_smem.wait()

    def send2(f, n, to):
        return pltpu.make_async_remote_copy(
            src_ref=ysend.at[f, to],
            dst_ref=y4[f].at[pl.ds(pl.multiple_of(n * 8, 8), 8)],
            send_sem=s2.at[f, to], recv_sem=r2.at[f, n],
            device_id=(blk, to), device_id_type=MESH,
        )

    def own2(f):
        return pltpu.make_async_copy(
            ysend.at[f, nar], y4[f].at[pl.ds(pl.multiple_of(nar * 8, 8), 8)], loc.at[6 + f]
        )

    w_rows = w_v[...].T
    w_parts = []
    for f in range(F):
        hi, lo = split(
            jnp.concatenate([w_rows[n * 32 + f * 8 : n * 32 + f * 8 + 8] for n in range(8)], axis=0)
        )
        w_parts.append((jnp.concatenate([hi, lo], axis=0), hi))

    get_own.wait()
    for step, other in NARROW:
        n = narrow_peer(step, other)
        send1(n, n).wait_recv()
    halves_x = [split(xt[:, half * 512 : half * 512 + 512]) for half in range(2)]
    for f in range(F):
        both, hi = w_parts[f]
        for half, (xh, xl) in enumerate(halves_x):
            y = nn_dot(both, xh)
            y = y[:64] + y[64:] + nn_dot(hi, xl)
            for b in range(4):
                scale = inv[half * 4 + b : half * 4 + b + 1, :]
                for n in range(8):
                    ysend[f, n, half * 4 + b] = (
                        y[n * 8 : n * 8 + 8, b * TILE : (b + 1) * TILE] * scale
                    )
        for step, other in NARROW:
            send2(f, nar, narrow_peer(step, other)).start()
        own2(f).start()

    get_list.wait()
    for step, other in ROW:
        send_list(step, other).wait_recv()
    for g in (2, 3):
        list_across(g).wait_recv()
    to_smem = pltpu.make_async_copy(lists_v, lists_s, loc.at[10])
    to_smem.start()
    to_smem.wait()

    def send_y(f):
        return pltpu.make_async_remote_copy(
            src_ref=y4[f], dst_ref=yp[f], send_sem=sy.at[f], recv_sem=ry.at[f],
            device_id=(partner, nar), device_id_type=MESH,
        )

    def send_blocks(buf, got, ssem, rsem, part, source, step, other):
        slot = step * 2 + other
        return pltpu.make_async_remote_copy(
            src_ref=buf.at[part, slot], dst_ref=got.at[part, source],
            send_sem=ssem.at[part, slot], recv_sem=rsem.at[part, source],
            device_id=(yh * 8 + row_peer(step, other), nar), device_id_type=MESH,
        )

    def column(slot, source, k):
        return lists_s[slot, source, k]

    def send_own(f, source, step, other):
        return send_blocks(own_b, got_own, so, ro, f, source, step, other)

    def send_early(f, source, step, other):
        return send_blocks(early_b, got_early, se, re, f, source, step, other)

    def send_late(level, source, step, other):
        first, wide = LEVELS[level]
        slot = step * 2 + other
        pairs = pl.ds(first // 2, wide // 2)
        return pltpu.make_async_remote_copy(
            src_ref=late_b.at[pairs, slot], dst_ref=got_late.at[pairs, source],
            send_sem=sq.at[level, slot], recv_sem=rq.at[level, source],
            device_id=(yh * 8 + row_peer(step, other), nar), device_id_type=MESH,
        )

    lane = lax.broadcasted_iota(jnp.int32, (8, TILE), 1)

    def swap_hub(source):
        return pltpu.make_async_remote_copy(
            src_ref=hub_v, dst_ref=hub_in.at[source], send_sem=sh.at[16], recv_sem=rh.at[source],
            device_id=(partner, nar), device_id_type=MESH,
        )

    def send_hub(src, source, sem, step, other):
        return pltpu.make_async_remote_copy(
            src_ref=src, dst_ref=hub_in.at[source], send_sem=sh.at[sem],
            recv_sem=rh.at[source],
            device_id=(yh * 8 + row_peer(step, other), nar), device_id_type=MESH,
        )

    rows_of = (ya, row1, row2, row3)

    def spread(step):
        return pltpu.make_async_remote_copy(
            src_ref=ya, dst_ref=rows_of[step], send_sem=sb.at[step], recv_sem=rb.at[step],
            device_id=(yh * 8 + row_peer(4 - step, 0), nar), device_id_type=MESH,
        )

    def relay(step):
        half = pl.ds(0 if step == 1 else 32, 32)
        return pltpu.make_async_remote_copy(
            src_ref=rows_of[step].at[half], dst_ref=row2.at[half],
            send_sem=sb.at[step - 1], recv_sem=rb.at[step - 1],
            device_id=(yh * 8 + row_peer(4 - step, 0), nar), device_id_type=MESH,
        )

    def send_first(g):
        return pltpu.make_async_remote_copy(
            src_ref=sel_b.at[g], dst_ref=got_first.at[g], send_sem=sf.at[g], recv_sem=rf.at[g],
            device_id=(chip[g], nar), device_id_type=MESH,
        )

    for f in range(F):
        own2(f).wait()
        for step, other in NARROW:
            n = narrow_peer(step, other)
            send2(f, n, n).wait_recv()
        if f == F - 1:
            hub = jnp.zeros((8, TILE), jnp.float32)
            for h in range(8):
                node = hubs[0, h]
                here = lane == lax.rem(node, TILE)
                for g in range(F):
                    col = jnp.sum(jnp.where(here, y4[g][node // TILE], 0.0), axis=1, keepdims=True)
                    hub = jnp.where(lane == g * 8 + h, col, hub)
            hub_v[...] = hub
            hub_in[blk] = hub
            swap_hub(blk).start()
            for step, other in ROW:
                send_hub(hub_v, blk, step * 2 + other, step, other).start()
        if f == 0:
            for step in (1, 3):
                spread(step).start()
            continue
        send_y(f).start()
        for step, other in ROW:
            slot = step * 2 + other
            for k in range(SLOTS):
                own_b[f - 1, slot, k] = y4[f][column(slot, blk, k)]
            send_own(f - 1, me, step, other).start()
        for k in range(SLOTS):
            got_own[f - 1, me, k] = y4[f][column(0, blk, k)]
        if f == 1:
            for step in (1, 3):
                spread(step).wait_recv()
                relay(step).start()

    for step in (1, 3):
        relay(step).wait_recv()
    for g, slot in ((2, 8), (3, 9), (1, 1), (0, 0)):
        for step in range(4):
            source = yh * 8 + row_peer(step, 0)
            for k in range(SLOTS):
                picked = rows_of[step][column(slot, source, k)]
                if g == 0:
                    got_first[g, step, k] = picked
                else:
                    sel_b[g, step, k] = picked
        if g > 0:
            send_first(g).start()

    def first_at(g, i, k):
        return got_first[g + lax.rem(i % 2 + core, 2), lax.rem(i // 2 - x + 4, 4), k]

    def keep_y(b, carry):
        for f in range(F):
            value[b, f] = y4[f][b]
        return carry

    lax.fori_loop(0, BLOCKS, keep_y, 0)
    swap_hub(partner).wait_recv()
    for step, other in ROW:
        send_hub(hub_in.at[partner], partner, 8 + step * 2 + other, step, other).start()

    send_y(1).wait_recv()
    for step, other in ROW:
        slot = step * 2 + other
        for k in range(SLOTS):
            early_b[0, slot, k] = yp[1][column(slot, partner, k)]
        send_early(0, me, step, other).start()
    for k in range(SLOTS):
        got_early[0, me, k] = yp[1][column(0, partner, k)]


    def product(xs, t):
        xh, xl = split(xs)
        x2 = jnp.concatenate(
            [
                jnp.concatenate([xh, xh], axis=1),
                jnp.concatenate([xl, jnp.zeros_like(xl)], axis=1),
            ],
            axis=0,
        )
        p = nt_dot(x2, t_v[t])
        return p[:32] + p[32:]

    def add(products, first):
        for j, p in enumerate(products):
            s = first + j
            back = order_s[s // TILE, lax.rem(s, TILE)]
            for f in range(F):
                value[BLOCKS + s, f] = p[f * 8 : f * 8 + 8, :] + value[back, f]

    def own_products(i, carry):
        for half in range(2):
            products = []
            for k in range(half * 8, half * 8 + 8):
                xs = jnp.concatenate([first_at(0, i, k)] + [got_own[f, i, k] for f in range(F - 1)], axis=0)
                products.append(product(xs, my_list[0, 2, yh * 8 + i, k]))
            add(products, i * 16 + half * 8)
        return carry

    def par_products(first, wide):
        def some(i, carry):
            products = []
            for j in range(8 // wide):
                source = i * (8 // wide) + j
                for k in range(first, first + wide):
                    xs = jnp.concatenate(
                        [first_at(2, source, k), got_early[0, source, k]]
                        + [got_late[k // 2, source, f, k % 2] for f in range(2)],
                        axis=0,
                    )
                    products.append(product(xs, my_list[0, 2, (1 - yh) * 8 + source, k]))
            add(products, 128 + first * 8 + i * 8)
            return carry

        lax.fori_loop(0, wide, some, 0)

    for f in range(2, F):
        send_y(f).wait_recv()

    def start_late(level):
        first, wide = LEVELS[level]
        for step, other in ROW:
            slot = step * 2 + other
            for k in range(first, first + wide):
                c = column(slot, partner, k)
                for f in range(2):
                    late_b[k // 2, slot, f, k % 2] = yp[2 + f][c]
            send_late(level, me, step, other).start()
        for k in range(first, first + wide):
            c = column(0, partner, k)
            for f in range(2):
                got_late[k // 2, me, f, k % 2] = yp[2 + f][c]

    def late_done(level):
        for step, other in ROW:
            send_late(level, row_peer(step, other), step, other).wait()

    for level in range(len(LEVELS)):
        start_late(level)
    for f in range(F - 1):
        for step, other in ROW:
            send_own(f, row_peer(step, other), step, other).wait()
    send_first(1).wait_recv()
    lax.fori_loop(0, 8, own_products, 0)

    for step, other in ROW:
        peer = row_peer(step, other)
        for o in (yh * 8 + peer, (1 - yh) * 8 + peer):
            send_hub(hub_v, o, 0, step, other).wait_recv()
    parts = []
    for f in range(F):
        total = jnp.zeros((8, TILE), jnp.float32)
        for o in range(16):
            moved = pltpu.roll(hub_in[o], (o * 8 - f * 8) % TILE, 1)
            total = jnp.where(lane // 8 == o, moved, total)
        parts.append(total)
    gh, gl = split(jnp.concatenate(parts, axis=0))
    g2 = jnp.concatenate([gh, gl], axis=0)
    get_hw.wait()

    def hub_sum(i, carry):
        hh, hl = split(hw_v[:, pl.ds(pl.multiple_of(i * 512, 512), 512)])
        p = nn_dot(g2, hh)
        p = p[:32] + p[32:] + nn_dot(gh, hl)
        for b in range(4):
            for f in range(F):
                hub_sums[i * 4 + b, f] = p[f * 8 : f * 8 + 8, b * TILE : (b + 1) * TILE]
        return carry

    lax.fori_loop(0, 16, hub_sum, 0)

    for f in range(F):
        if f > 0:
            send_y(f).wait_send()
        for step, other in NARROW:
            n = narrow_peer(step, other)
            send2(f, n, n).wait_send()
    for step, other in NARROW:
        n = narrow_peer(step, other)
        send1(n, n).wait_send()
    for step, other in ROW:
        send_list(step, other).wait_send()
    for g in (2, 3):
        list_across(g).wait_send()
    swap_hub(partner).wait_send()
    for step, other in ROW:
        send_hub(hub_v, blk, step * 2 + other, step, other).wait_send()
        send_hub(hub_v, blk, 8 + step * 2 + other, step, other).wait_send()
    for step, other in ROW:
        send_early(0, row_peer(step, other), step, other).wait()
    for step in (1, 3):
        spread(step).wait_send()
        relay(step).wait_send()
    for g in (1, 2, 3):
        send_first(g).wait_send()
    for g in (2, 3):
        send_first(g).wait_recv()
    for level in range(len(LEVELS)):
        late_done(level)
        par_products(*LEVELS[level])

    sub = lax.broadcasted_iota(jnp.int32, (8, TILE), 0)
    biases = []
    for f in range(F):
        column_f = jnp.zeros((8, TILE), jnp.float32)
        for i in range(8):
            column_f = jnp.where(sub == i, bias[nar * 32 + f * 8 + i], column_f)
        biases.append(column_f)

    def finish(i, carry):
        inv = lax.rsqrt(deg_v[pl.ds(pl.multiple_of(i * 8, 8), 8), :].astype(jnp.float32))
        for b in range(8):
            end = order_s[8, i * 8 + b]
            for f in range(F):
                out[f * 8 : f * 8 + 8, pl.ds(pl.multiple_of((i * 8 + b) * TILE, TILE), TILE)] = (
                    jnp.maximum(
                        (value[end, f] + hub_sums[i * 8 + b, f]) * inv[b : b + 1, :] + biases[f],
                        0.0,
                    )
                )
        return carry

    lax.fori_loop(0, 8, finish, 0)


def exchange(feat, deg, weight, lists, counts, hubs, bias, tiles, hub_w):
    f32, bf16 = jnp.float32, jnp.bfloat16
    dma = pltpu.SemaphoreType.DMA
    vmem = pltpu.VMEM
    smem = pl.BlockSpec(memory_space=pltpu.SMEM)
    hbm = pl.BlockSpec(memory_space=pl.ANY)
    tile = (8, TILE)
    return pl.pallas_call(
        exchange_kernel,
        out_shape=pltpu.VMEM((32, BLOCKS * TILE), f32),
        in_specs=[hbm, hbm, hbm, hbm, smem, smem, smem, smem, hbm, hbm],
        out_specs=pl.BlockSpec(memory_space=vmem),
        scratch_shapes=[
            vmem((256, 1024), f32),
            vmem((F, 8, 8, *tile), f32),
            *[vmem((BLOCKS, *tile), f32)] * 7,
            vmem((F - 1, 8, SLOTS, *tile), f32),
            vmem((1, 8, SLOTS, *tile), f32),
            vmem((8, 8, 2, 2, *tile), f32),
            *[vmem((BLOCKS, *tile), f32)] * 3,
            vmem((4, 4, SLOTS, *tile), f32),
            vmem((4, 4, SLOTS, *tile), f32),
            vmem((F - 1, 8, SLOTS, *tile), f32),
            vmem((1, 8, SLOTS, *tile), f32),
            vmem((8, 8, 2, 2, *tile), f32),
            vmem((10, 16, SLOTS), jnp.int32),
            pltpu.SMEM((10, 16, SLOTS), jnp.int32),
            vmem(tile, f32),
            vmem((16, *tile), f32),
            vmem((BLOCKS, TILE), jnp.int32),
            vmem((256, 256), f32),
            vmem((2, 64, TILE, TILE), f32),
            vmem((TV, TILE, 2 * TILE), bf16),
            vmem((128, BLOCKS * TILE), f32),
            vmem((16, TILE), jnp.int32),
            pltpu.SMEM((16, TILE), jnp.int32),
            vmem((BLOCKS + TV, F, *tile), f32),
            vmem((BLOCKS, F, *tile), f32),
            dma((8,)), dma((8,)),
            dma((F, 8)), dma((F, 8)),
            dma((F,)), dma((F,)),
            dma((10,)), dma((10,)),
            dma((17,)), dma((16,)),
            dma((F - 1, 8)), dma((F - 1, 8)),
            dma((1, 8)), dma((1, 8)),
            dma((len(LEVELS), 8)), dma((len(LEVELS), 8)),
            dma((4,)), dma((4,)),
            dma((4,)), dma((4,)),
            dma((16,)),
        ],
        compiler_params=pltpu.CompilerParams(
            collective_id=0, has_side_effects=True, vmem_limit_bytes=60 * 2**20
        ),
    )(feat, deg, weight, lists, lists, counts, hubs, bias, tiles, hub_w)


def body(
    features, degrees, tile_values, tile_list, tile_count, hub_local, hub_weights, weight, out_bias
):
    deg = degrees.reshape(BLOCKS, TILE)
    lists = jnp.transpose(tile_list, (0, 2, 1, 3))
    return exchange(
        features, deg, weight, lists, tile_count, hub_local, out_bias, tile_values, hub_weights
    )


def solution(mesh):
    return jax.shard_map(
        body,
        mesh=mesh,
        in_specs=(
            P("narrow", "blk"),
            P("blk"),
            P("blk", None, None),
            P("blk", None, None, None),
            P("blk", None),
            P("blk", None),
            P(None, "blk"),
            P(),
            P(),
        ),
        out_specs=P("narrow", "blk"),
        check_vma=False,
    )
```
